32 devices in a mesh: groups: 2 (over x), rows: 16 (over z, y, core).
Axes of the slice: x: 2, y: 2, z: 4, core: 2. Of those that a mesh axis runs over, the one named last changes fastest.
Arguments:
- tiles: bfloat16 [256, 40, 128, 128], P(('groups', 'rows')), parts along dimension 0
- pattern: int32 [256, 40], P(('groups', 'rows')), parts along dimension 0, may hold values from 0 to 127, as said below
- basis: float32 [32768, 256], P(('groups', 'rows')), parts along dimension 0, may hold values from -3 to 3
Outputs:
- modes: float32 [32768, 256], P(('groups', 'rows')), parts along dimension 0
- projected: float32 [4, 256, 256], P('groups'), parts along dimension 0
The draws below stay inside these ranges and needn't reach their ends.
There are 2 independent parts, one for each index of `groups`. The reference program is written for one: setup_inputs(seed, part) draws one part's arguments, and reference() takes and returns one part's arrays. A program takes and returns all parts, laid end to end along the dimension named above; each array names one. Nothing has to cross between parts.
Inputs may be any that keep to these rules, and one draw needn't show every extreme that they name: The column blocks of one block row are distinct; one of them is the row itself and every other lies within 24 blocks of it, counted cyclically over 128 block rows. The pattern is symmetric: block row r names c exactly when c names r, and tiles hold C's symmetric blocks (the tile at (c, r) is the transpose of the tile at (r, c)). Row r names r + d and r - d for the same set of distances in every block row, plus its partner in the pairing of 2 i with 2 i + 1; the slots are in no fixed order.
All inputs are finite; a program needn't handle non-finite values.
Results may differ from the reference program's by a relative error of at most 0.0041.
Values may be sent and summed in bfloat16 or wider, within the bound.
No kernel may reach another device: no remote copies, remote signals or barrier semaphores. Data moves between devices by JAX's collectives and lax.ppermute only.
A program may use at most 128 MiB of HBM per device.

```python
import math
import jax
import jax.numpy as jnp
from jax import lax

TILE = 128
MODES = 256
NNZ = 40
BR = 8
STEPS = 2
NB = 128
ORDER = 16384


def layout(key):
    half = (NNZ - 2) // 2
    span = 3 * BR
    dist_key = jax.random.fold_in(key, 101)
    slot_key = jax.random.fold_in(key, 102)
    scores = jax.random.randint(dist_key, (span - 1,), 0, 2 ** 20, dtype=jnp.int32) * 512 + jnp.arange(span - 1, dtype=jnp.int32)
    order_idx = jnp.argsort(scores, stable=True)
    distances = (order_idx[:half] + 2).astype(jnp.int32)
    slot_scores = jax.random.randint(slot_key, (NB, NNZ), 0, 2 ** 20, dtype=jnp.int32) * 64 + jnp.arange(NNZ, dtype=jnp.int32)[None, :]
    slot_order = jnp.argsort(slot_scores, axis=1, stable=True).astype(jnp.int32)
    return (distances, slot_order)


def noise_of(key, shape):
    return jax.random.normal(key, shape, jnp.float32)


def draw_pattern(key, part):
    distances, slot_order = layout(key)
    row_ids = jnp.arange(NB, dtype=jnp.int32)[:, None]
    partner = jnp.where(row_ids % 2 == 0, row_ids + 1, row_ids - 1)
    canon = jnp.concatenate([row_ids, partner, row_ids + distances[None, :], row_ids - distances[None, :]], axis=1)
    canon = jnp.mod(canon, NB).astype(jnp.int32)
    return jnp.take_along_axis(canon, slot_order, axis=1).astype(jnp.int32)


def draw_tiles(key, part):
    distances, slot_order = layout(key)
    key = jax.random.fold_in(key, 11)
    half = (NNZ - 2) // 2
    spread = 0.5 / math.sqrt(NNZ * TILE)
    diag_key = jax.random.fold_in(key, 1)
    pair_key = jax.random.fold_in(key, 2)
    fwd_key = jax.random.fold_in(key, 3)
    raw_diag = noise_of(diag_key, (NB, TILE, TILE))
    diag_tiles = (raw_diag + jnp.swapaxes(raw_diag, 1, 2)) * (spread / math.sqrt(2.0)) + 1.5 * jnp.eye(TILE, dtype=jnp.float32)[None, :, :]
    pair_tiles = noise_of(pair_key, (NB // 2, TILE, TILE)) * spread
    row_ids = jnp.arange(NB, dtype=jnp.int32)
    pair_rows = jnp.take(pair_tiles, row_ids // 2, axis=0)
    odd_rows = (row_ids % 2 == 1)[:, None, None]
    partner_tiles = jnp.where(odd_rows, jnp.swapaxes(pair_rows, 1, 2), pair_rows)
    forward = noise_of(fwd_key, (NB, half, TILE, TILE)) * spread
    back_rows = jnp.mod(row_ids[:, None] - distances[None, :], NB).astype(jnp.int32)
    slot_ids = jnp.arange(half, dtype=jnp.int32)[None, :]
    backward = jnp.swapaxes(forward[back_rows, slot_ids], 2, 3)
    canon = jnp.concatenate([diag_tiles[:, None], partner_tiles[:, None], forward, backward], axis=1)
    ordered = jnp.take_along_axis(canon, slot_order[:, :, None, None], axis=1)
    return ordered.astype(jnp.bfloat16)


def draw_basis(key, part):
    key = jax.random.fold_in(key, 23)
    own_key = jax.random.fold_in(key, 1)
    shared_key = jax.random.fold_in(key, 2)
    shared = jnp.clip(jax.random.normal(shared_key, (ORDER, 1), jnp.float32), -3.0, 3.0)
    own = jnp.clip(jax.random.normal(own_key, (ORDER, MODES), jnp.float32), -3.0, 3.0)
    mixed = 0.7 * own + 0.3 * shared
    lowest = jnp.min(mixed)
    highest = jnp.max(mixed)
    return (-3.0 + 6.0 * ((mixed - lowest) / (highest - lowest))).astype(jnp.float32)


def setup_inputs(seed: int = 0, part: int = 0) -> dict:
    splits = jax.random.split(jax.random.key(seed), 4)
    part_keys = jax.random.split(jax.random.fold_in(splits[3], part), 4)
    return {
        "tiles": draw_tiles(jax.random.fold_in(jax.random.fold_in(splits[3], part), 71), part),
        "pattern": draw_pattern(jax.random.fold_in(jax.random.fold_in(splits[3], part), 71), part),
        "basis": draw_basis(jax.random.fold_in(jax.random.fold_in(splits[3], part), 71), part),
    }


def reference(tiles, pattern, basis):
    current = basis
    projected_list = []
    for step_index in range(STEPS):
        rounded = current.astype(jnp.bfloat16)
        blocks = rounded.reshape(NB, TILE, MODES)

        def row_block(pair):
            tile_row, columns = pair
            picked = jnp.take(blocks, columns.astype(jnp.int32), axis=0).astype(jnp.float32)
            return jnp.einsum('kij,kjm->im', tile_row.astype(jnp.float32), picked)
        product = lax.map(row_block, (tiles, pattern)).reshape(ORDER, MODES)
        wide = rounded.astype(jnp.float32)
        gram = jnp.einsum('rm,rn->mn', product, product, precision=lax.Precision.HIGHEST)
        projected_list.append(jnp.einsum('rm,rn->mn', wide, product, precision=lax.Precision.HIGHEST))
        lower = jnp.linalg.cholesky(gram)
        inverse = lax.linalg.triangular_solve(lower, jnp.eye(MODES, dtype=jnp.float32), left_side=True, lower=True)
        current = jnp.einsum('rm,nm->rn', product, inverse, precision=lax.Precision.HIGHEST)
    return (current * math.sqrt(ORDER), jnp.stack(projected_list))
```

```python
import functools
import math

import jax
import jax.numpy as jnp
from jax import lax
from jax.experimental import pallas as pl
from jax.experimental.pallas import tpu as pltpu
from jax.sharding import PartitionSpec as P

STEPS = 2
HIGHEST = lax.Precision.HIGHEST
B = 8
LANES = 128
MIB = 2**20


def permuted(value, target):
    peers = lax.axis_size("rows")
    return lax.ppermute(value, "rows", [(i, target(i) % peers) for i in range(peers)])


def neighbourhood(blocks):
    before = permuted(blocks, lambda i: i + 2)
    after = permuted(blocks, lambda i: i - 2)
    far = permuted(blocks, lambda i: i + 3 if i % 2 else i - 3)
    other = lambda v: permuted(v, lambda i: i ^ 1)
    return [blocks, other(blocks), before, other(before), after, other(after), far]


def places(pattern, block_rows):
    peers = lax.axis_size("rows")
    me = lax.axis_index("rows")
    owner = pattern // block_rows
    apart = jnp.mod(owner // 2 - me // 2 + 2, peers // 2) - 2
    crossed = (owner % 2 != me % 2).astype(jnp.int32)
    piece = jnp.where(apart == 0, crossed, jnp.where(apart == -1, 2 + crossed, jnp.where(apart == 1, 4 + crossed, 6)))
    return piece * block_rows + pattern % block_rows


def summed(value):
    peers = lax.axis_size("rows")
    if peers & (peers - 1):
        return lax.psum(value, "rows")
    core = lax.axis_index("rows") % 2
    half = value.shape[0] // 2
    mine = lax.dynamic_slice_in_dim(value, core * half, half)
    rest = lax.dynamic_slice_in_dim(value, (1 - core) * half, half)
    mine = mine + permuted(rest, lambda i: i ^ 1)
    step = 2
    while step < peers:
        mine = mine + permuted(mine, lambda i: i ^ step)
        step *= 2
    rest = permuted(mine, lambda i: i ^ 1)
    return jnp.where(core == 0, jnp.concatenate([mine, rest]), jnp.concatenate([rest, mine]))


def product_kernel(place_ref, tiles_ref, *refs, pieces):
    piece_refs, (out_ref, low_ref, window, sems) = refs[:pieces], refs[pieces:]
    r = pl.program_id(0)
    block_rows = piece_refs[0].shape[0]

    @pl.when(r == 0)
    def _():
        copies = [
            pltpu.make_async_copy(piece_refs[i], window.at[pl.ds(i * block_rows, block_rows)], sems.at[i])
            for i in range(pieces)
        ]
        for c in copies:
            c.start()
        for c in copies:
            c.wait()

    total = None
    for k in range(0, tiles_ref.shape[1], 2):
        left = jnp.concatenate([tiles_ref[0, k], tiles_ref[0, k + 1]], axis=1)
        right = jnp.concatenate([window[place_ref[r, k]], window[place_ref[r, k + 1]]], axis=0)
        term = jnp.dot(left, right, preferred_element_type=jnp.float32)
        total = term if total is None else total + term
    out_ref[...] = total
    low_ref[...] = total.astype(jnp.bfloat16)


def product_of(place, tiles, pieces):
    block_rows, slots, tile, _ = tiles.shape
    modes = pieces[0].shape[-1]
    n = len(pieces)
    rows = block_rows * tile
    return pl.pallas_call(
        functools.partial(product_kernel, pieces=n),
        grid_spec=pltpu.PrefetchScalarGridSpec(
            num_scalar_prefetch=1,
            grid=(block_rows,),
            in_specs=[pl.BlockSpec((1, slots, tile, tile), lambda r, s: (r, 0, 0, 0))]
            + [pl.BlockSpec(memory_space=pl.ANY)] * n,
            out_specs=[pl.BlockSpec((tile, modes), lambda r, s: (r, 0))] * 2,
            scratch_shapes=[pltpu.VMEM((n * block_rows, tile, modes), jnp.bfloat16), pltpu.SemaphoreType.DMA((n,))],
        ),
        out_shape=[
            jax.ShapeDtypeStruct((rows, modes), jnp.float32),
            jax.ShapeDtypeStruct((rows, modes), jnp.bfloat16),
        ],
        cost_estimate=pl.CostEstimate(
            flops=2 * rows * slots * tile * modes, bytes_accessed=2 * tiles.size, transcendentals=0
        ),
        compiler_params=pltpu.CompilerParams(vmem_limit_bytes=20 * MIB),
    )(place, tiles, *[p.reshape(block_rows, tile, modes) for p in pieces])


def dot(a, b, dims=((1,), (0,))):
    return lax.dot_general(a, b, (dims, ((), ())), precision=HIGHEST, preferred_element_type=jnp.float32)


def pack(full, out_ref):
    h = full.shape[0] // 2
    out_ref[0:h, :] = full[:h, :h]
    out_ref[h : 2 * h, :] = full[h:, :h]
    out_ref[2 * h : 3 * h, :] = full[h:, h:]


def unpacked(ref):
    h = ref.shape[0] // 3
    a, b, d = ref[0:h, :], ref[h : 2 * h, :], ref[2 * h : 3 * h, :]
    return jnp.concatenate([jnp.concatenate([a, b.T], axis=1), jnp.concatenate([b, d], axis=1)], axis=0)


def first_sums_kernel(product_ref, rounded_ref, gram_ref, proj_ref):
    product = product_ref[...]
    pack(dot(product, product, ((0,), (0,))), gram_ref)
    pack(dot(rounded_ref[...].astype(jnp.float32), product, ((0,), (0,))), proj_ref)


def later_sums_kernel(raw_ref, sent_ref, inverse_ref, product_ref, gram_ref, proj_ref):
    inverse = inverse_ref[...]
    product = dot(raw_ref[...], inverse, ((1,), (1,)))
    product_ref[...] = product
    pack(dot(product, product, ((0,), (0,))), gram_ref)
    pack(dot(inverse, dot(sent_ref[...].astype(jnp.float32), product, ((0,), (0,)))), proj_ref)


def on_chip(kernel, out_shape, *args, flops=0):
    return pl.pallas_call(
        kernel,
        out_shape=out_shape,
        cost_estimate=pl.CostEstimate(flops=flops, bytes_accessed=2**20, transcendentals=0),
        compiler_params=pltpu.CompilerParams(vmem_limit_bytes=24 * MIB),
    )(*args)


def lane_bcast(x, j):
    return jnp.take_along_axis(x, jnp.full(x.shape, j, jnp.int32), axis=1)

def sub_bcast(x, i):
    return jnp.broadcast_to(x[i:i+1, :], x.shape)

def wide(x, n):
    return x if n == 1 else jnp.concatenate([x] * n, axis=1)

def reciprocal(x):
    return 1.0 / x

def rsqrt(x):
    y = lax.rsqrt(x)
    return y * (1.5 - 0.5 * x * y * y)

def inverse_factor(g):
    n = g.shape[0]
    groups, tiles = n // B, n // LANES
    row = lax.broadcasted_iota(jnp.int32, (n, n), 0)
    lane_n = lax.broadcasted_iota(jnp.int32, (n, n), 1)
    diagonal = jnp.where(row == lane_n, g, 0.0)
    scale_row = rsqrt(jnp.sum(diagonal, axis=0, keepdims=True))
    scale_col = rsqrt(jnp.sum(diagonal, axis=1, keepdims=True))
    g = g * scale_col * scale_row
    x = [g[B*k:B*k+B, :] for k in range(groups)]
    lane = lax.broadcasted_iota(jnp.int32, (B, n), 1)
    sub = lax.broadcasted_iota(jnp.int32, (B, n), 0)
    for k in range(groups - 1):
        t = B * k // LANES
        at = B * k % LANES
        tile = slice(t * LANES, (t + 1) * LANES)
        here = lane // B == k
        cols = [lane_bcast(x[k][:, tile], at + j) for j in range(B)]
        p = [[sub_bcast(cols[j], i) for j in range(B)] for i in range(B)]
        start = jnp.where(here, jnp.where(lane - B * k == sub, 1.0, 0.0), x[k])
        rows = [sub_bcast(start, i) for i in range(B)]
        for a in range(0, B, 2):
            b = a + 1
            inv = reciprocal(p[a][a] * p[b][b] - p[a][b] * p[a][b])
            i00, i01, i11 = p[b][b] * inv, -p[a][b] * inv, p[a][a] * inv
            w00, w01, w11 = wide(i00, tiles), wide(i01, tiles), wide(i11, tiles)
            rows[a], rows[b] = w00 * rows[a] + w01 * rows[b], w01 * rows[a] + w11 * rows[b]
            for j in range(b + 1, B):
                p[a][j], p[b][j] = i00 * p[a][j] + i01 * p[b][j], i01 * p[a][j] + i11 * p[b][j]
            for i in range(B):
                if i in (a, b):
                    continue
                ca, cb = p[i][a], p[i][b]
                rows[i] = rows[i] - (wide(ca, tiles) * rows[a] + wide(cb, tiles) * rows[b])
                for j in range(b + 1, B):
                    p[i][j] = p[i][j] - (ca * p[a][j] + cb * p[b][j])
        for i in range(k + 1, groups):
            c = [wide(lane_bcast(x[i][:, tile], at + j), tiles) for j in range(B)]
            s = [c[j] * rows[j] for j in range(B)]
            s = ((s[0] + s[1]) + (s[2] + s[3])) + ((s[4] + s[5]) + (s[6] + s[7]))
            x[i] = jnp.where(here, 0.0, x[i]) - s
    strip = jnp.zeros((B, n), jnp.float32)
    for k in range(groups):
        strip = jnp.where(lane // B == k, x[k], strip)
    w8 = []
    sub1 = sub[:, :LANES]
    lane1 = lane[:, :LANES]
    for t in range(tiles):
        d = strip[:, t * LANES:(t + 1) * LANES]
        base = lane1 // B * B
        cols = [jnp.take_along_axis(d, base + j, axis=1) for j in range(B)]
        p = [[sub_bcast(cols[j], i) for j in range(B)] for i in range(B)]
        m = [[None] * B for _ in range(B)]
        pivots = []
        for a in range(B):
            pivots.append(p[a][a])
            inv = reciprocal(p[a][a])
            for i in range(a + 1, B):
                l = p[i][a] * inv
                for j in range(a + 1, i + 1):
                    p[i][j] = p[i][j] - l * p[j][a]
                for j in range(a):
                    m[i][j] = m[i][j] - l * m[a][j]
                m[i][a] = -l
        out = jnp.zeros((B, LANES), jnp.float32)
        for i in range(B):
            r = rsqrt(pivots[i])
            for j in range(i + 1):
                v = r if i == j else r * m[i][j]
                out = jnp.where((sub1 == i) & (lane1 % B == j), v, out)
        w8.append(out)
    result = []
    for k in range(groups):
        t, at = B * k // LANES, B * k % LANES
        here = lane // B == k
        start = jnp.where(lane < B * k, x[k], jnp.where(here & (lane - B * k == sub), 1.0, 0.0))
        s = [wide(lane_bcast(w8[t], at + j), tiles) * sub_bcast(start, j) for j in range(B)]
        s = ((s[0] + s[1]) + (s[2] + s[3])) + ((s[4] + s[5]) + (s[6] + s[7]))
        result.append(s)
    return jnp.concatenate(result, axis=0) * scale_row

def inverse_kernel(gram_ref, inverse_ref):
    inverse_ref[...] = inverse_factor(unpacked(gram_ref))


def modes_kernel(scale, gram_ref, product_ref, modes_ref):
    inverse = inverse_factor(unpacked(gram_ref)) * scale
    modes_ref[...] = dot(product_ref[...], inverse, ((1,), (1,)))


def symmetric(packed):
    h = packed.shape[0] // 3
    a, b, d = packed[:h], packed[h : 2 * h], packed[2 * h :]
    return jnp.concatenate([jnp.concatenate([a, b.T], axis=1), jnp.concatenate([b, d], axis=1)], axis=0)


def per_device(tiles, pattern, basis):
    block_rows, _, tile, _ = tiles.shape
    rows, modes = basis.shape
    order = rows * lax.axis_size("rows")
    f32 = lambda *shape: jax.ShapeDtypeStruct(shape, jnp.float32)
    packed = f32(3 * modes // 2, modes // 2)
    chain = 200_000_000
    place = places(pattern, block_rows)

    rounded = basis.astype(jnp.bfloat16)
    product, sent = product_of(place, tiles, neighbourhood(rounded))
    pieces = neighbourhood(sent)
    gram, proj = on_chip(first_sums_kernel, (packed, packed), product, rounded, flops=24 * rows * modes * modes)
    gram, first = summed(gram), summed(proj)
    inverse = on_chip(inverse_kernel, f32(modes, modes), gram, flops=chain)

    raw, _ = product_of(place, tiles, pieces)
    product, gram, proj = on_chip(
        later_sums_kernel, (f32(rows, modes), packed, packed), raw, sent, inverse, flops=36 * rows * modes * modes
    )
    gram, second = summed(gram), summed(proj)
    out = on_chip(functools.partial(modes_kernel, math.sqrt(order)), f32(rows, modes), gram, product, flops=chain)
    return out, jnp.stack([symmetric(first), symmetric(second)])


def solution(mesh):
    placed = (
        P(("groups", "rows"), None, None, None),
        P(("groups", "rows"), None),
        P(("groups", "rows"), None),
    )
    return jax.shard_map(
        per_device,
        mesh=mesh,
        in_specs=placed,
        out_specs=(P(("groups", "rows"), None), P("groups", None, None)),
        check_vma=False,
    )
```

```python
import functools
import math

import jax
import jax.numpy as jnp
from jax import lax
from jax.experimental import pallas as pl
from jax.experimental.pallas import tpu as pltpu
from jax.sharding import PartitionSpec as P

STEPS = 2
HIGHEST = lax.Precision.HIGHEST
B = 8
LANES = 128
MIB = 2**20


def permuted(value, target):
    peers = lax.axis_size("rows")
    return lax.ppermute(value, "rows", [(i, target(i) % peers) for i in range(peers)])


def neighbourhood(blocks):
    before = permuted(blocks, lambda i: i + 2)
    after = permuted(blocks, lambda i: i - 2)
    far = permuted(blocks, lambda i: i + 3 if i % 2 else i - 3)
    other = lambda v: permuted(v, lambda i: i ^ 1)
    return [blocks, other(blocks), before, other(before), after, other(after), far]


def places(pattern, block_rows):
    peers = lax.axis_size("rows")
    me = lax.axis_index("rows")
    owner = pattern // block_rows
    apart = jnp.mod(owner // 2 - me // 2 + 2, peers // 2) - 2
    crossed = (owner % 2 != me % 2).astype(jnp.int32)
    piece = jnp.where(apart == 0, crossed, jnp.where(apart == -1, 2 + crossed, jnp.where(apart == 1, 4 + crossed, 6)))
    return piece * block_rows + pattern % block_rows


def summed(value):
    peers = lax.axis_size("rows")
    if peers & (peers - 1):
        return lax.psum(value, "rows")
    core = lax.axis_index("rows") % 2
    half = value.shape[0] // 2
    mine = lax.dynamic_slice_in_dim(value, core * half, half)
    rest = lax.dynamic_slice_in_dim(value, (1 - core) * half, half)
    mine = mine + permuted(rest, lambda i: i ^ 1)
    step = 2
    while step < peers:
        mine = mine + permuted(mine, lambda i: i ^ step)
        step *= 2
    rest = permuted(mine, lambda i: i ^ 1)
    return jnp.where(core == 0, jnp.concatenate([mine, rest]), jnp.concatenate([rest, mine]))


def product_kernel(place_ref, tiles_ref, *refs, pieces):
    piece_refs, (out_ref, low_ref, window, held, sems, row_sems) = refs[:pieces], refs[pieces:]
    block_rows, tile = piece_refs[0].shape[:2]
    copies = [
        pltpu.make_async_copy(piece_refs[i], window.at[pl.ds(i * block_rows, block_rows)], sems.at[i])
        for i in range(pieces)
    ]
    row_copies = [pltpu.make_async_copy(tiles_ref.at[r], held.at[r], row_sems.at[r]) for r in range(block_rows)]
    row_copies[0].start()
    for c in copies:
        c.start()
    for c in row_copies[1:]:
        c.start()
    for c in copies:
        c.wait()
    for r in range(block_rows):
        row_copies[r].wait()
        total = None
        for k in range(0, tiles_ref.shape[1], 2):
            left = jnp.concatenate([held[r, k], held[r, k + 1]], axis=1)
            right = jnp.concatenate([window[place_ref[r, k]], window[place_ref[r, k + 1]]], axis=0)
            term = jnp.dot(left, right, preferred_element_type=jnp.float32)
            total = term if total is None else total + term
        out_ref[r * tile : (r + 1) * tile, :] = total
        low_ref[r * tile : (r + 1) * tile, :] = total.astype(jnp.bfloat16)


def product_of(place, tiles, pieces):
    block_rows, slots, tile, _ = tiles.shape
    modes = pieces[0].shape[-1]
    n = len(pieces)
    rows = block_rows * tile
    return pl.pallas_call(
        functools.partial(product_kernel, pieces=n),
        in_specs=[pl.BlockSpec(memory_space=pltpu.SMEM), pl.BlockSpec(memory_space=pltpu.HBM)]
        + [pl.BlockSpec(memory_space=pl.ANY)] * n,
        scratch_shapes=[
            pltpu.VMEM((n * block_rows, tile, modes), jnp.bfloat16),
            pltpu.VMEM(tiles.shape, jnp.bfloat16),
            pltpu.SemaphoreType.DMA((n,)),
            pltpu.SemaphoreType.DMA((block_rows,)),
        ],
        out_shape=[
            jax.ShapeDtypeStruct((rows, modes), jnp.float32),
            jax.ShapeDtypeStruct((rows, modes), jnp.bfloat16),
        ],
        cost_estimate=pl.CostEstimate(
            flops=2 * rows * slots * tile * modes, bytes_accessed=2 * tiles.size, transcendentals=0
        ),
        compiler_params=pltpu.CompilerParams(vmem_limit_bytes=32 * MIB),
    )(place, tiles, *[p.reshape(block_rows, tile, modes) for p in pieces])


def dot(a, b, dims=((1,), (0,))):
    return lax.dot_general(a, b, (dims, ((), ())), precision=HIGHEST, preferred_element_type=jnp.float32)


def pack(full, out_ref):
    h = full.shape[0] // 2
    out_ref[0:h, :] = full[:h, :h]
    out_ref[h : 2 * h, :] = full[h:, :h]
    out_ref[2 * h : 3 * h, :] = full[h:, h:]


def unpacked(ref):
    h = ref.shape[0] // 3
    a, b, d = ref[0:h, :], ref[h : 2 * h, :], ref[2 * h : 3 * h, :]
    return jnp.concatenate([jnp.concatenate([a, b.T], axis=1), jnp.concatenate([b, d], axis=1)], axis=0)


def sums_kernel(product_ref, rounded_ref, gram_ref, proj_ref):
    product = product_ref[...]
    pack(dot(product, product, ((0,), (0,))), gram_ref)
    pack(dot(rounded_ref[...].astype(jnp.float32), product, ((0,), (0,))), proj_ref)


def on_chip(kernel, out_shape, *args, flops=0):
    return pl.pallas_call(
        kernel,
        out_shape=out_shape,
        cost_estimate=pl.CostEstimate(flops=flops, bytes_accessed=2**20, transcendentals=0),
        compiler_params=pltpu.CompilerParams(vmem_limit_bytes=24 * MIB),
    )(*args)


def lane_bcast(x, j):
    return jnp.take_along_axis(x, jnp.full(x.shape, j, jnp.int32), axis=1)

def sub_bcast(x, i):
    return jnp.broadcast_to(x[i:i+1, :], x.shape)

def wide(x, n):
    return x if n == 1 else jnp.concatenate([x] * n, axis=1)

def reciprocal(x):
    return 1.0 / x

def rsqrt(x):
    y = lax.rsqrt(x)
    return y * (1.5 - 0.5 * x * y * y)

def inverse_factor(g):
    n = g.shape[0]
    groups, tiles = n // B, n // LANES
    row = lax.broadcasted_iota(jnp.int32, (n, n), 0)
    lane_n = lax.broadcasted_iota(jnp.int32, (n, n), 1)
    diagonal = jnp.where(row == lane_n, g, 0.0)
    scale_row = rsqrt(jnp.sum(diagonal, axis=0, keepdims=True))
    scale_col = rsqrt(jnp.sum(diagonal, axis=1, keepdims=True))
    g = g * scale_col * scale_row
    x = [g[B*k:B*k+B, :] for k in range(groups)]
    lane = lax.broadcasted_iota(jnp.int32, (B, n), 1)
    sub = lax.broadcasted_iota(jnp.int32, (B, n), 0)
    for k in range(groups - 1):
        t = B * k // LANES
        at = B * k % LANES
        tile = slice(t * LANES, (t + 1) * LANES)
        here = lane // B == k
        cols = [lane_bcast(x[k][:, tile], at + j) for j in range(B)]
        p = [[sub_bcast(cols[j], i) for j in range(B)] for i in range(B)]
        start = jnp.where(here, jnp.where(lane - B * k == sub, 1.0, 0.0), x[k])
        rows = [sub_bcast(start, i) for i in range(B)]
        for a in range(0, B, 2):
            b = a + 1
            inv = reciprocal(p[a][a] * p[b][b] - p[a][b] * p[a][b])
            i00, i01, i11 = p[b][b] * inv, -p[a][b] * inv, p[a][a] * inv
            w00, w01, w11 = wide(i00, tiles), wide(i01, tiles), wide(i11, tiles)
            rows[a], rows[b] = w00 * rows[a] + w01 * rows[b], w01 * rows[a] + w11 * rows[b]
            for j in range(b + 1, B):
                p[a][j], p[b][j] = i00 * p[a][j] + i01 * p[b][j], i01 * p[a][j] + i11 * p[b][j]
            for i in range(B):
                if i in (a, b):
                    continue
                ca, cb = p[i][a], p[i][b]
                rows[i] = rows[i] - (wide(ca, tiles) * rows[a] + wide(cb, tiles) * rows[b])
                for j in range(b + 1, B):
                    p[i][j] = p[i][j] - (ca * p[a][j] + cb * p[b][j])
        for i in range(k + 1, groups):
            c = [wide(lane_bcast(x[i][:, tile], at + j), tiles) for j in range(B)]
            s = [c[j] * rows[j] for j in range(B)]
            s = ((s[0] + s[1]) + (s[2] + s[3])) + ((s[4] + s[5]) + (s[6] + s[7]))
            x[i] = jnp.where(here, 0.0, x[i]) - s
    strip = jnp.zeros((B, n), jnp.float32)
    for k in range(groups):
        strip = jnp.where(lane // B == k, x[k], strip)
    w8 = []
    sub1 = sub[:, :LANES]
    lane1 = lane[:, :LANES]
    for t in range(tiles):
        d = strip[:, t * LANES:(t + 1) * LANES]
        base = lane1 // B * B
        cols = [jnp.take_along_axis(d, base + j, axis=1) for j in range(B)]
        p = [[sub_bcast(cols[j], i) for j in range(B)] for i in range(B)]
        m = [[None] * B for _ in range(B)]
        pivots = []
        for a in range(B):
            pivots.append(p[a][a])
            inv = reciprocal(p[a][a])
            for i in range(a + 1, B):
                l = p[i][a] * inv
                for j in range(a + 1, i + 1):
                    p[i][j] = p[i][j] - l * p[j][a]
                for j in range(a):
                    m[i][j] = m[i][j] - l * m[a][j]
                m[i][a] = -l
        out = jnp.zeros((B, LANES), jnp.float32)
        for i in range(B):
            r = rsqrt(pivots[i])
            for j in range(i + 1):
                v = r if i == j else r * m[i][j]
                out = jnp.where((sub1 == i) & (lane1 % B == j), v, out)
        w8.append(out)
    result = []
    for k in range(groups):
        t, at = B * k // LANES, B * k % LANES
        here = lane // B == k
        start = jnp.where(lane < B * k, x[k], jnp.where(here & (lane - B * k == sub), 1.0, 0.0))
        s = [wide(lane_bcast(w8[t], at + j), tiles) * sub_bcast(start, j) for j in range(B)]
        s = ((s[0] + s[1]) + (s[2] + s[3])) + ((s[4] + s[5]) + (s[6] + s[7]))
        result.append(s)
    return jnp.concatenate(result, axis=0) * scale_row

def inverse_kernel(gram_ref, inverse_ref):
    inverse_ref[...] = inverse_factor(unpacked(gram_ref))


def modes_kernel(scale, gram_ref, product_ref, modes_ref):
    inverse = inverse_factor(unpacked(gram_ref)) * scale
    modes_ref[...] = dot(product_ref[...], inverse, ((1,), (1,)))


def symmetric(packed):
    h = packed.shape[0] // 3
    a, b, d = packed[:h], packed[h : 2 * h], packed[2 * h :]
    return jnp.concatenate([jnp.concatenate([a, b.T], axis=1), jnp.concatenate([b, d], axis=1)], axis=0)


def sandwich_kernel(inverse_ref, proj_ref, out_ref):
    inverse = inverse_ref[...]
    out_ref[...] = dot(dot(inverse, unpacked(proj_ref)), inverse, ((1,), (1,)))


def per_device(tiles, pattern, basis):
    block_rows, _, tile, _ = tiles.shape
    rows, modes = basis.shape
    order = rows * lax.axis_size("rows")
    f32 = lambda *shape: jax.ShapeDtypeStruct(shape, jnp.float32)
    packed = f32(3 * modes // 2, modes // 2)
    chain = 200_000_000
    place = places(pattern, block_rows)

    rounded = basis.astype(jnp.bfloat16)
    product, sent = product_of(place, tiles, neighbourhood(rounded))
    pieces = neighbourhood(sent)
    sums = 16 * rows * modes * modes
    gram, proj = on_chip(sums_kernel, (packed, packed), product, rounded, flops=sums)
    gram, first = summed(gram), summed(proj)

    raw, _ = product_of(place, tiles, pieces)
    raw_gram, proj = on_chip(sums_kernel, (packed, packed), raw, sent, flops=sums)
    raw_gram, second = summed(raw_gram), summed(proj)
    inverse = on_chip(inverse_kernel, f32(modes, modes), gram, flops=chain)
    out = on_chip(functools.partial(modes_kernel, math.sqrt(order)), f32(rows, modes), raw_gram, raw, flops=chain)
    second = on_chip(sandwich_kernel, f32(modes, modes), inverse, second)
    return out, jnp.stack([symmetric(first), second])


def solution(mesh):
    placed = (
        P(("groups", "rows"), None, None, None),
        P(("groups", "rows"), None),
        P(("groups", "rows"), None),
    )
    return jax.shard_map(
        per_device,
        mesh=mesh,
        in_specs=placed,
        out_specs=(P(("groups", "rows"), None), P("groups", None, None)),
        check_vma=False,
    )
```

```python
import functools
import math

import jax
import jax.numpy as jnp
from jax import lax
from jax.experimental import pallas as pl
from jax.experimental.pallas import tpu as pltpu
from jax.sharding import PartitionSpec as P

B = 8
LANES = 128
CHUNK = 8
MIB = 2**20


def permuted(value, target):
    peers = lax.axis_size("rows")
    return lax.ppermute(value, "rows", [(i, target(i) % peers) for i in range(peers)])


def swapped(value):
    return permuted(value, lambda i: i ^ 1)


def after(value, *others):
    return lax.optimization_barrier((value, others))[0]


def neighbourhood(blocks, meanwhile, then=lambda made: made):
    before = permuted(blocks, lambda i: i + 2)
    behind = permuted(blocks, lambda i: i - 2)
    made = meanwhile()
    later = after(blocks, made)
    far = permuted(later, lambda i: i + 3 if i % 2 else i - 3)
    made = then(made)
    before, behind = after((before, behind), made)
    return [blocks, swapped(later), before, swapped(before), behind, swapped(behind), far], made


def kernel_call(kernel, out_shape, *args, flops=0, limit=16, **kwargs):
    return pl.pallas_call(
        kernel,
        out_shape=out_shape,
        cost_estimate=pl.CostEstimate(flops=flops, bytes_accessed=2**20, transcendentals=0),
        compiler_params=pltpu.CompilerParams(vmem_limit_bytes=limit * MIB),
        **kwargs,
    )(*args)


def prepare_kernel(pattern_ref, basis_ref, place_ref, rounded_ref, *, block_rows, peers):
    rounded_ref[...] = basis_ref[...].astype(jnp.bfloat16)
    me = lax.axis_index("rows")
    pattern = pattern_ref[...]
    owner = lax.div(pattern, block_rows)
    apart = lax.rem(lax.div(owner, 2) - lax.div(me, 2) + (2 + peers // 2), peers // 2) - 2
    crossed = lax.rem(owner + me, 2)
    piece = jnp.where(apart == 0, crossed, jnp.where(apart == -1, 2 + crossed, jnp.where(apart == 1, 4 + crossed, 6)))
    place_ref[...] = piece * block_rows + lax.rem(pattern, block_rows)


def held_kernel(tiles_ref, held_ref, sems):
    copies = [pltpu.make_async_copy(tiles_ref.at[r], held_ref.at[r], sems.at[r]) for r in range(tiles_ref.shape[0])]
    for c in copies:
        c.start()
    for c in copies:
        c.wait()


def held(tiles):
    return pl.pallas_call(
        held_kernel,
        in_specs=[pl.BlockSpec(memory_space=pltpu.HBM)],
        out_specs=pl.BlockSpec(memory_space=pltpu.VMEM),
        scratch_shapes=[pltpu.SemaphoreType.DMA((tiles.shape[0],))],
        out_shape=jax.ShapeDtypeStruct(tiles.shape, tiles.dtype),
        cost_estimate=pl.CostEstimate(flops=0, bytes_accessed=4 * tiles.size, transcendentals=0),
        compiler_params=pltpu.CompilerParams(vmem_limit_bytes=14 * MIB),
    )(tiles)


def product_kernel(place_ref, tiles_ref, *refs, pieces):
    piece_refs, (out_ref, low_ref, window) = refs[:pieces], refs[pieces:]
    block_rows, tile = piece_refs[0].shape[:2]
    for i in range(pieces):
        window[i * block_rows : (i + 1) * block_rows] = piece_refs[i][...]
    for r in range(block_rows):
        total = None
        for k in range(0, tiles_ref.shape[1], 2):
            left = jnp.concatenate([tiles_ref[r, k], tiles_ref[r, k + 1]], axis=1)
            right = jnp.concatenate([window[place_ref[r, k]], window[place_ref[r, k + 1]]], axis=0)
            term = jnp.dot(left, right, preferred_element_type=jnp.float32)
            total = term if total is None else total + term
        out_ref[r * tile : (r + 1) * tile, :] = total
        low_ref[r * tile : (r + 1) * tile, :] = total.astype(jnp.bfloat16)


def product_of(place, tiles, pieces):
    block_rows, slots, tile, _ = tiles.shape
    modes = pieces[0].shape[-1]
    n = len(pieces)
    rows = block_rows * tile
    return pl.pallas_call(
        functools.partial(product_kernel, pieces=n),
        in_specs=[pl.BlockSpec(memory_space=pltpu.SMEM)] + [pl.BlockSpec(memory_space=pltpu.VMEM)] * (n + 1),
        scratch_shapes=[pltpu.VMEM((n * block_rows, tile, modes), jnp.bfloat16)],
        out_shape=[
            jax.ShapeDtypeStruct((rows, modes), jnp.float32),
            jax.ShapeDtypeStruct((rows, modes), jnp.bfloat16),
        ],
        cost_estimate=pl.CostEstimate(
            flops=2 * rows * slots * tile * modes, bytes_accessed=2 * tiles.size, transcendentals=0
        ),
        compiler_params=pltpu.CompilerParams(vmem_limit_bytes=12 * MIB),
    )(place, tiles, *[p.reshape(block_rows, tile, modes) for p in pieces])


def dot(a, b, dims=((1,), (0,))):
    return lax.dot_general(a, b, (dims, ((), ())), precision=lax.Precision.HIGHEST, preferred_element_type=jnp.float32)


def write_sums(product_ref, rounded_ref, out_refs):
    down = ((0,), (0,))
    h = product_ref.shape[1] // 2
    pa, pb = product_ref[:, :h], product_ref[:, h:]
    xa, xb = rounded_ref[:, :h].astype(jnp.float32), rounded_ref[:, h:].astype(jnp.float32)
    core = lax.rem(lax.axis_index("rows"), 2)
    for (mine_ref, rest_ref), la, lb in ((out_refs[:2], pa, pb), (out_refs[-2:], xa, xb)):
        low, mid, high = dot(la, pa, down), dot(lb, pa, down), dot(lb, pb, down)
        first = jnp.concatenate([low, mid[: h // 2]], axis=0)
        last = jnp.concatenate([mid[h // 2 :], high], axis=0)
        to = slice(None) if len(out_refs) == 4 else slice(0, 3 * h // 2) if la is pa else slice(3 * h // 2, 3 * h)
        mine_ref[to, :] = jnp.where(core == 0, first, last)
        rest_ref[to, :] = jnp.where(core == 0, last, first)


def first_sums_kernel(product_ref, rounded_ref, *out_refs):
    write_sums(product_ref, rounded_ref, out_refs)


def later_sums_kernel(product_ref, rounded_ref, a_ref, b_ref, added_ref, *out_refs):
    write_sums(product_ref, rounded_ref, out_refs)
    added_ref[...] = a_ref[...] + b_ref[...]


def added_kernel(a_ref, b_ref, out_ref):
    out_ref[...] = a_ref[...] + b_ref[...]


def added(a, b):
    return kernel_call(added_kernel, jax.ShapeDtypeStruct(a.shape, a.dtype), a, b, limit=4)


def summed(mine, rest, first=1, last=None):
    step = first
    while step < (last or lax.axis_size("rows")):
        mine = added(mine, permuted(rest if step == 1 else mine, lambda i: i ^ step))
        step *= 2
    return mine


def unpacked(mine, rest):
    core = lax.rem(lax.axis_index("rows"), 2)
    first, last = jnp.where(core == 0, mine, rest), jnp.where(core == 0, rest, mine)
    h = 2 * mine.shape[0] // 3
    a, d = first[:h], last[h // 2 :]
    b = jnp.concatenate([first[h:], last[: h // 2]], axis=0)
    return jnp.concatenate([jnp.concatenate([a, b.T], axis=1), jnp.concatenate([b, d], axis=1)], axis=0)


def lane_bcast(x, j):
    return jnp.take_along_axis(x, jnp.broadcast_to(j, x.shape).astype(jnp.int32), axis=1)


def sub_bcast(x, i):
    return jnp.broadcast_to(x[i : i + 1, :], x.shape)


def wide(x, n):
    return x if n == 1 else jnp.concatenate([x] * n, axis=1)


def rsqrt(x):
    y = lax.rsqrt(x)
    return y * (1.5 - 0.5 * x * y * y)


def tree(terms):
    while len(terms) > 1:
        terms = [a + b for a, b in zip(terms[::2], terms[1::2])]
    return terms[0]


def pivot_rows(xk, k, tile, at, lane, sub, tiles):
    here = lane // B == k
    cols = [lane_bcast(xk[:, tile], at + j) for j in range(B)]
    p = [[None] * B for i in range(B)]
    for i in range(B):
        for j in range(i, B):
            p[i][j] = p[j][i] = sub_bcast(cols[j], i)
    start = jnp.where(here, jnp.where(lane - B * k == sub, 1.0, 0.0), xk)
    rows = [sub_bcast(start, i) for i in range(B)]
    for a in range(0, B, 2):
        b, c, d = a + 1, a + 2, a + 3
        if a % 4 == 0:
            det = p[a][a] * p[b][b] - p[a][b] * p[a][b]
            inv = 1.0 / det
            i00, i01, i11 = p[b][b] * inv, -p[a][b] * inv, p[a][a] * inv
            def schur(i, j):
                left = p[b][b] * p[a][j] - p[a][b] * p[b][j]
                right = p[a][a] * p[b][j] - p[a][b] * p[a][j]
                return det * p[i][j] - (p[i][a] * left + p[i][b] * right)

            scc, scd, sdd = schur(c, c), schur(c, d), schur(d, d)
            follow = det / (scc * sdd - scd * scd)
        else:
            i00, i01, i11 = sdd * follow, -scd * follow, scc * follow
        w00, w01, w11 = wide(i00, tiles), wide(i01, tiles), wide(i11, tiles)
        rows[a], rows[b] = w00 * rows[a] + w01 * rows[b], w01 * rows[a] + w11 * rows[b]
        for j in range(b + 1, B):
            p[a][j], p[b][j] = i00 * p[a][j] + i01 * p[b][j], i01 * p[a][j] + i11 * p[b][j]
        for i in range(B):
            if i in (a, b):
                continue
            ca, cb = p[i][a], p[i][b]
            rows[i] = rows[i] - (wide(ca, tiles) * rows[a] + wide(cb, tiles) * rows[b])
            for j in range(b + 1, B):
                p[i][j] = p[i][j] - (ca * p[a][j] + cb * p[b][j])
    return rows


def pivot_factors(d, sub, lane):
    base = lane // B * B
    cols = [jnp.take_along_axis(d, base + j, axis=1) for j in range(B)]
    p = [[sub_bcast(cols[j], i) for j in range(B)] for i in range(B)]
    m = [[None] * B for _ in range(B)]
    out = jnp.zeros(d.shape, jnp.float32)
    for a in range(B):
        inv = 1.0 / p[a][a]
        for i in range(a + 1, B):
            l = p[i][a] * inv
            for j in range(a + 1, i + 1):
                p[i][j] = p[i][j] - l * p[j][a]
            for j in range(a):
                m[i][j] = m[i][j] - l * m[a][j]
            m[i][a] = -l
    for i in range(B):
        r = rsqrt(p[i][i])
        for j in range(i + 1):
            out = jnp.where((sub == i) & (lane % B == j), r if i == j else r * m[i][j], out)
    return out


def eliminated_block(x, first, groups, lane, sub, tiles):
    acting = []
    for s in range(groups):
        k = first + s
        t = k * B // LANES
        tile, at = slice(t * LANES, (t + 1) * LANES), k * B - t * LANES
        here = lane // B == k
        rows = pivot_rows(x[s], k, tile, at, lane, sub, tiles)
        for i in range(s + 1, groups):
            c = [wide(lane_bcast(x[i][:, tile], at + j), tiles) for j in range(B)]
            x[i] = jnp.where(here, 0.0, x[i]) - tree([c[j] * rows[j] for j in range(B)])
        own = rows[0]
        for j in range(1, B):
            own = jnp.where(sub == j, rows[j], own)
        acting.append(jnp.where((lane // B > k) & (lane // B < first + groups), 0.0, own))
    return x, acting


def inverse_factors(grams):
    n = grams[0].shape[0]
    tiles, many, per = n // LANES, range(len(grams)), CHUNK
    lane = lax.broadcasted_iota(jnp.int32, (B, n), 1)
    sub = lax.broadcasted_iota(jnp.int32, (B, n), 0)
    row = lax.broadcasted_iota(jnp.int32, (n, n), 0)
    all_lanes = lax.broadcasted_iota(jnp.int32, (n, n), 1)
    rest, scales, done = [], [], [[] for _ in many]
    for g in grams:
        d = jnp.where(row == all_lanes, g, 0.0)
        scales.append(rsqrt(jnp.sum(d, axis=0, keepdims=True)))
        rest.append(g * rsqrt(jnp.sum(d, axis=1, keepdims=True)) * scales[-1])
    for first in range(0, n // B, per):
        size = per * B
        lo = first * B
        both = [
            eliminated_block([rest[m][i * B : i * B + B, :] for i in range(per)], first, per, lane, sub, tiles)
            for m in many
        ]
        for m in many:
            x, acting = both[m]
            done[m] += x
            if lo + size < n:
                left = jnp.concatenate(x, axis=0)
                below = (lo + size) // LANES * LANES
                update = dot(left[:, below:], jnp.concatenate(acting, axis=0), ((0,), (0,)))[lo + size - below :]
                inside = all_lanes[lo + size :] // size == lo // size
                rest[m] = jnp.where(inside, 0.0, rest[m][size:]) - update
    result = []
    for m in many:
        strip = done[m][0]
        for k in range(1, n // B):
            strip = jnp.where(lane // B == k, done[m][k], strip)
        factors = [pivot_factors(strip[:, t * LANES : (t + 1) * LANES], sub[:, :LANES], lane[:, :LANES]) for t in range(tiles)]
        out = []
        for k in range(n // B):
            t, at = k * B // LANES, k * B % LANES
            unit = jnp.where((lane // B == k) & (lane - B * k == sub), 1.0, 0.0)
            start = jnp.where(lane < B * k, done[m][k], unit)
            out.append(tree([wide(lane_bcast(factors[t], at + j), tiles) * sub_bcast(start, j) for j in range(B)]))
        result.append(jnp.concatenate(out, axis=0) * scales[m])
    return result


def modes_kernel(first_ref, first_rest_ref, raw_ref, raw_rest_ref, product_ref, modes_ref, inverse_ref, *, scale):
    n = raw_ref.shape[0]
    first = unpacked(first_ref[:n, :], first_rest_ref[:n, :])
    inverse, both = inverse_factors([first, unpacked(raw_ref[...], raw_rest_ref[...])])
    h = both.shape[0] // 2
    along = ((1,), (1,))
    both = both * scale
    modes_ref[:, :h] = dot(product_ref[:, :h], both[:h, :h], along)
    modes_ref[:, h:] = dot(product_ref[...], both[h:, :], along)
    inverse_ref[...] = inverse


def projected_kernel(first_ref, first_rest_ref, proj_ref, proj_rest_ref, inverse_ref, projected_ref):
    n = proj_ref.shape[0]
    inverse = inverse_ref[...]
    projected_ref[0] = unpacked(first_ref[n:, :], first_rest_ref[n:, :])
    proj = unpacked(proj_ref[...], proj_rest_ref[...])
    projected_ref[1] = dot(dot(inverse, proj), inverse, ((1,), (1,)))


def per_device(tiles, pattern, basis):
    block_rows, _, tile, _ = tiles.shape
    rows, modes = basis.shape
    peers = lax.axis_size("rows")
    shape = jax.ShapeDtypeStruct
    half_sum = 3 * modes // 4
    flops = 12 * rows * modes * modes
    place, rounded = kernel_call(
        functools.partial(prepare_kernel, block_rows=block_rows, peers=peers),
        (shape(pattern.shape, jnp.int32), shape((rows, modes), jnp.bfloat16)),
        pattern, basis,
        limit=8,
    )
    pieces, tiles = neighbourhood(rounded, lambda: held(tiles))
    product, sent = product_of(place, tiles, pieces)
    both = (shape((2 * half_sum, modes // 2), jnp.float32),) * 2
    pieces, first = neighbourhood(
        sent,
        lambda: summed(*kernel_call(first_sums_kernel, both, product, rounded, flops=flops), 1, 2),
        lambda made: summed(made, None, 2, 4),
    )
    partner = permuted(first, lambda i: i ^ 4)

    raw, _ = product_of(place, tiles, pieces)
    single = (shape((half_sum, modes // 2), jnp.float32),) * 4
    first, gram, gram_rest, proj, proj_rest = kernel_call(
        later_sums_kernel, (both[0],) + single, raw, sent, first, partner, flops=flops
    )
    first = summed(first, None, 8)
    first_rest = swapped(first)
    gram, proj = summed(gram, gram_rest), summed(proj, proj_rest)
    modes_out, inverse = kernel_call(
        functools.partial(modes_kernel, scale=math.sqrt(rows * peers)),
        (shape((rows, modes), jnp.float32), shape((modes, modes), jnp.float32)),
        first, first_rest, gram, swapped(gram), raw,
        flops=4_000_000_000,
    )
    projected = kernel_call(
        projected_kernel, shape((2, modes, modes), jnp.float32), first, first_rest, proj, swapped(proj), inverse
    )
    return modes_out, projected


def solution(mesh):
    placed = (
        P(("groups", "rows"), None, None, None),
        P(("groups", "rows"), None),
        P(("groups", "rows"), None),
    )
    return jax.shard_map(
        per_device,
        mesh=mesh,
        in_specs=placed,
        out_specs=(P(("groups", "rows"), None), P("groups", None, None)),
        check_vma=False,
    )
```

```python
import functools
import math

import jax
import jax.numpy as jnp
from jax import lax
from jax.experimental import pallas as pl
from jax.experimental.pallas import tpu as pltpu
from jax.sharding import PartitionSpec as P

B = 8
LANES = 128
CHUNK = 8
MIB = 2**20
LONG = 8_000_000_000


def permuted(value, target):
    peers = lax.axis_size("rows")
    return lax.ppermute(value, "rows", [(i, target(i) % peers) for i in range(peers)])


def swapped(value):
    return permuted(value, lambda i: i ^ 1)


def after(value, *others):
    return lax.optimization_barrier((value, others))[0]


def neighbourhood(blocks, meanwhile, then=lambda made: made):
    before = permuted(blocks, lambda i: i + 2)
    behind = permuted(blocks, lambda i: i - 2)
    far = permuted(blocks, lambda i: i + 3 if i % 2 else i - 3)
    made = meanwhile()
    other = swapped(after(blocks, made))
    made = then(made)
    before, behind = after(before, made), after(behind, made)
    return [blocks, other, before, swapped(before), behind, swapped(behind), far], made


def kernel_call(kernel, out_shape, *args, flops=0, limit=16, **kwargs):
    return pl.pallas_call(
        kernel,
        out_shape=out_shape,
        cost_estimate=pl.CostEstimate(flops=flops, bytes_accessed=2**20, transcendentals=0),
        compiler_params=pltpu.CompilerParams(vmem_limit_bytes=limit * MIB),
        **kwargs,
    )(*args)


def prepare_kernel(pattern_ref, basis_ref, place_ref, rounded_ref, held, sems, *, block_rows, peers):
    parts = sems.shape[0]
    step = basis_ref.shape[0] // parts
    at = [slice(i * step, (i + 1) * step) for i in range(parts)]
    copies = [pltpu.make_async_copy(basis_ref.at[at[i]], held.at[at[i]], sems.at[i]) for i in range(parts)]
    for c in copies:
        c.start()
    for i in range(parts):
        copies[i].wait()
        rounded_ref[at[i], :] = held[at[i], :].astype(jnp.bfloat16)
    me = lax.axis_index("rows")
    pattern = pattern_ref[...]
    owner = lax.div(pattern, block_rows)
    apart = lax.rem(lax.div(owner, 2) - lax.div(me, 2) + (2 + peers // 2), peers // 2) - 2
    crossed = lax.rem(owner + me, 2)
    piece = jnp.where(apart == 0, crossed, jnp.where(apart == -1, 2 + crossed, jnp.where(apart == 1, 4 + crossed, 6)))
    place_ref[...] = piece * block_rows + lax.rem(pattern, block_rows)


def held_kernel(tiles_ref, held_ref, turn_ref, sems):
    copies = [pltpu.make_async_copy(tiles_ref.at[r], held_ref.at[r], sems.at[r]) for r in range(tiles_ref.shape[0])]
    for c in copies:
        c.start()
    n = turn_ref.shape[0]
    both = lax.broadcasted_iota(jnp.int32, (n, n), 0) & lax.broadcasted_iota(jnp.int32, (n, n), 1)
    shift = 1
    while 2**shift < n:
        both = both ^ (both >> shift)
        shift *= 2
    turn_ref[...] = jnp.where(both & 1 == 0, 1.0, -1.0).astype(turn_ref.dtype) * (1.0 / math.sqrt(n))
    for c in copies:
        c.wait()


def held(tiles, modes):
    return pl.pallas_call(
        held_kernel,
        in_specs=[pl.BlockSpec(memory_space=pltpu.HBM)],
        out_specs=[pl.BlockSpec(memory_space=pltpu.VMEM)] * 2,
        scratch_shapes=[pltpu.SemaphoreType.DMA((tiles.shape[0],))],
        out_shape=[
            jax.ShapeDtypeStruct(tiles.shape, tiles.dtype),
            jax.ShapeDtypeStruct((modes, modes), jnp.bfloat16),
        ],
        cost_estimate=pl.CostEstimate(flops=0, bytes_accessed=4 * tiles.size, transcendentals=0),
        compiler_params=pltpu.CompilerParams(vmem_limit_bytes=14 * MIB),
    )(tiles)


def turned(x, turn, parts):
    total = None
    for _ in range(parts):
        part = x.astype(jnp.bfloat16)
        term = jnp.dot(part, turn, preferred_element_type=jnp.float32)
        total = term if total is None else total + term
        x = x - part.astype(jnp.float32)
    return total


def product_kernel(place_ref, tiles_ref, turn_ref, *refs, pieces):
    piece_refs, (product_ref, *sent_refs, window) = refs[:pieces], refs[pieces:]
    block_rows, tile = piece_refs[0].shape[:2]
    for i in range(pieces):
        window[i * block_rows : (i + 1) * block_rows] = piece_refs[i][...]
    for r in range(block_rows):
        total = None
        for k in range(0, tiles_ref.shape[1], 2):
            left = jnp.concatenate([tiles_ref[r, k], tiles_ref[r, k + 1]], axis=1)
            right = jnp.concatenate([window[place_ref[r, k]], window[place_ref[r, k + 1]]], axis=0)
            term = jnp.dot(left, right, preferred_element_type=jnp.float32)
            total = term if total is None else total + term
        product_ref[r * tile : (r + 1) * tile, :] = total
    if sent_refs:
        sent_refs[0][...] = turned(product_ref[...], turn_ref[...], 2).astype(sent_refs[0].dtype)
    else:
        product_ref[...] = turned(product_ref[...], turn_ref[...], 3)


def product_of(place, tiles, turn, pieces, *types):
    block_rows, slots, tile, _ = tiles.shape
    modes = pieces[0].shape[-1]
    n = len(pieces)
    rows = block_rows * tile
    return pl.pallas_call(
        functools.partial(product_kernel, pieces=n),
        in_specs=[pl.BlockSpec(memory_space=pltpu.SMEM)] + [pl.BlockSpec(memory_space=pltpu.VMEM)] * (n + 2),
        scratch_shapes=[pltpu.VMEM((n * block_rows, tile, modes), jnp.bfloat16)],
        out_shape=[jax.ShapeDtypeStruct((rows, modes), t) for t in types],
        cost_estimate=pl.CostEstimate(flops=LONG, bytes_accessed=2 * tiles.size, transcendentals=0),
        compiler_params=pltpu.CompilerParams(vmem_limit_bytes=12 * MIB),
    )(place, tiles, turn, *[p.reshape(block_rows, tile, modes) for p in pieces])


def dot(a, b, dims=((1,), (0,))):
    return lax.dot_general(a, b, (dims, ((), ())), precision=lax.Precision.HIGHEST, preferred_element_type=jnp.float32)


def my_bit(bit):
    return lax.rem(lax.div(lax.axis_index("rows"), bit), 2)


def halves(left, right):
    down = ((0,), (0,))
    h = right.shape[1] // 2
    la, lb, ra, rb = left[:, :h], left[:, h:], right[:, :h], right[:, h:]
    low, mid, high = dot(la, ra, down), dot(lb, ra, down), dot(lb, rb, down)
    first = jnp.concatenate([low, mid[: h // 2]], axis=0)
    last = jnp.concatenate([mid[h // 2 :], high], axis=0)
    core = my_bit(1)
    return jnp.where(core == 0, first, last), jnp.where(core == 0, last, first)


def first_sums_kernel(product_ref, rounded_ref, mine_ref, rest_ref):
    n = mine_ref.shape[0] // 2
    product = product_ref[...]
    mine_ref[:n, :], rest_ref[:n, :] = halves(product, product)
    mine_ref[n:, :], rest_ref[n:, :] = halves(rounded_ref[...].astype(jnp.float32), product)


def gram_kernel(product_ref, a_ref, b_ref, mine_ref, rest_ref, added_ref):
    product = product_ref[...]
    mine_ref[...], rest_ref[...] = halves(product, product)
    added_ref[...] = a_ref[...] + b_ref[...]


def proj_kernel(product_ref, sent_ref, turn_ref, mine_ref, rest_ref):
    rounded = jnp.dot(sent_ref[...], turn_ref[...], preferred_element_type=jnp.float32)
    mine_ref[...], rest_ref[...] = halves(rounded, product_ref[...])


def split_kernel(a_ref, b_ref, mine_ref, rest_ref):
    total = a_ref[...] + b_ref[...]
    n = total.shape[0] // 2
    bit = my_bit(2)
    mine_ref[...] = jnp.where(bit == 0, total[:n], total[n:])
    rest_ref[...] = jnp.where(bit == 0, total[n:], total[:n])


def added_kernel(a_ref, b_ref, out_ref):
    out_ref[...] = a_ref[...] + b_ref[...]


def added(a, b):
    return kernel_call(added_kernel, jax.ShapeDtypeStruct(a.shape, a.dtype), a, b, limit=4)


def summed(mine, rest, first=1, last=None):
    step = first
    while step < (last or lax.axis_size("rows")):
        mine = added(mine, permuted(rest if step == 1 else mine, lambda i: i ^ step))
        step *= 2
    return mine


def unpacked(mine, rest):
    core = my_bit(1)
    first, last = jnp.where(core == 0, mine, rest), jnp.where(core == 0, rest, mine)
    h = 2 * mine.shape[0] // 3
    a, d = first[:h], last[h // 2 :]
    b = jnp.concatenate([first[h:], last[: h // 2]], axis=0)
    return jnp.concatenate([jnp.concatenate([a, b.T], axis=1), jnp.concatenate([b, d], axis=1)], axis=0)


def lane_bcast(x, j):
    return jnp.take_along_axis(x, jnp.broadcast_to(j, x.shape).astype(jnp.int32), axis=1)


def sub_bcast(x, i):
    return jnp.broadcast_to(x[i : i + 1, :], x.shape)


def wide(x, n):
    return x if n == 1 else jnp.concatenate([x] * n, axis=1)


def rsqrt(x):
    y = lax.rsqrt(x)
    return y * (1.5 - 0.5 * x * y * y)


def tree(terms):
    while len(terms) > 1:
        terms = [a + b for a, b in zip(terms[::2], terms[1::2])]
    return terms[0]


def pivot_rows(xk, k, tile, at, lane, sub, tiles):
    here = lane // B == k
    cols = [lane_bcast(xk[:, tile], at + j) for j in range(B)]
    start = jnp.where(here, jnp.where(lane - B * k == sub, 1.0, 0.0), xk)
    x = start
    one = sub[:, :LANES]
    for a in range(0, B, 2):
        b = a + 1
        pa = [sub_bcast(cols[j], a) for j in range(B)]
        pb = [sub_bcast(cols[j], b) for j in range(B)]
        inv = 1.0 / (pa[a] * pb[b] - pa[b] * pa[b])
        i00, i01, i11 = pb[b] * inv, -pa[b] * inv, pa[a] * inv
        mine = (one == a) | (one == b)
        ra, rb = sub_bcast(x, a), sub_bcast(x, b)
        qa = wide(i00, tiles) * ra + wide(i01, tiles) * rb
        qb = wide(i01, tiles) * ra + wide(i11, tiles) * rb
        ca = jnp.where(mine, jnp.where(one == a, -1.0, 0.0), cols[a])
        cb = jnp.where(mine, jnp.where(one == b, -1.0, 0.0), cols[b])
        wm = wide(mine, tiles)
        x = jnp.where(wm, 0.0, x) - (wide(ca, tiles) * qa + wide(cb, tiles) * qb)
        for j in range(b + 1, B):
            ta, tb = i00 * pa[j] + i01 * pb[j], i01 * pa[j] + i11 * pb[j]
            cols[j] = jnp.where(mine, 0.0, cols[j]) - (ca * ta + cb * tb)
    return [sub_bcast(x, i) for i in range(B)]


def pivot_factors(d, sub, lane):
    base = lane // B * B
    cols = [jnp.take_along_axis(d, base + j, axis=1) for j in range(B)]
    p = [[sub_bcast(cols[j], i) for j in range(B)] for i in range(B)]
    m = [[None] * B for _ in range(B)]
    out = jnp.zeros(d.shape, jnp.float32)
    for a in range(B):
        inv = 1.0 / p[a][a]
        for i in range(a + 1, B):
            l = p[i][a] * inv
            for j in range(a + 1, i + 1):
                p[i][j] = p[i][j] - l * p[j][a]
            for j in range(a):
                m[i][j] = m[i][j] - l * m[a][j]
            m[i][a] = -l
    for i in range(B):
        r = rsqrt(p[i][i])
        for j in range(i + 1):
            out = jnp.where((sub == i) & (lane % B == j), r if i == j else r * m[i][j], out)
    return out


def eliminated_block(x, first, groups, lane, sub, tiles):
    acting = []
    for s in range(groups):
        k = first + s
        t = k * B // LANES
        tile, at = slice(t * LANES, (t + 1) * LANES), k * B - t * LANES
        here = lane // B == k
        rows = pivot_rows(x[s], k, tile, at, lane, sub, tiles)
        for i in range(s + 1, groups):
            c = [wide(lane_bcast(x[i][:, tile], at + j), tiles) for j in range(B)]
            x[i] = jnp.where(here, 0.0, x[i]) - tree([c[j] * rows[j] for j in range(B)])
        own = rows[0]
        for j in range(1, B):
            own = jnp.where(sub == j, rows[j], own)
        acting.append(jnp.where((lane // B > k) & (lane // B < first + groups), 0.0, own))
    return x, acting


def scaled(g):
    row = lax.broadcasted_iota(jnp.int32, g.shape, 0)
    d = jnp.where(row == lax.broadcasted_iota(jnp.int32, g.shape, 1), g, 0.0)
    scale = rsqrt(jnp.sum(d, axis=0, keepdims=True))
    return g * rsqrt(jnp.sum(d, axis=1, keepdims=True)) * scale, scale


def eliminated(rest, first, last):
    n = rest[0].shape[1]
    tiles, many, per = n // LANES, range(len(rest)), CHUNK
    lane = lax.broadcasted_iota(jnp.int32, (B, n), 1)
    sub = lax.broadcasted_iota(jnp.int32, (B, n), 0)
    rest, done = list(rest), [[] for _ in many]
    for start in range(first, last, per):
        size, lo = per * B, start * B
        both = [
            eliminated_block([rest[m][i * B : i * B + B, :] for i in range(per)], start, per, lane, sub, tiles)
            for m in many
        ]
        for m in many:
            x, acting = both[m]
            done[m] += x
            if lo + size < n:
                left = jnp.concatenate(x, axis=0)
                below = (lo + size) // LANES * LANES
                update = dot(left[:, below:], jnp.concatenate(acting, axis=0), ((0,), (0,)))[lo + size - below :]
                lanes = lax.broadcasted_iota(jnp.int32, update.shape, 1)
                rest[m] = jnp.where(lanes // size == lo // size, 0.0, rest[m][size:]) - update
    return [jnp.concatenate(d, axis=0) for d in done], rest


def inverse_factor(done, scale):
    n = done.shape[0]
    lane = lax.broadcasted_iota(jnp.int32, (B, n), 1)
    sub = lax.broadcasted_iota(jnp.int32, (B, n), 0)
    groups = [done[k * B : k * B + B, :] for k in range(n // B)]
    strip = groups[0]
    for k in range(1, n // B):
        strip = jnp.where(lane // B == k, groups[k], strip)
    factors = [
        pivot_factors(strip[:, t : t + LANES], sub[:, :LANES], lane[:, :LANES]) for t in range(0, n, LANES)
    ]
    spread = jnp.concatenate(factors, axis=1)
    blocks, unit = [], []
    for k in range(n // B):
        here = lane // B == k
        blocks.append(jnp.where(here, spread, 0.0))
        eye = jnp.where(here & (lane - B * k == sub), 1.0, 0.0)
        unit.append(jnp.where(lane < B * k, groups[k], eye))
    return dot(jnp.concatenate(blocks, axis=0), jnp.concatenate(unit, axis=0)) * scale


def upper_kernel(
    keep_ref, other_ref, keep_rest_ref, other_rest_ref, raw_ref, raw_rest_ref, done_ref, rest_ref, scale_ref
):
    bit = my_bit(2)
    mine = jnp.where(bit == 0, keep_ref[...], other_ref[...])
    rest = jnp.where(bit == 0, keep_rest_ref[...], other_rest_ref[...])
    one, scale_ref[0:1, :] = scaled(unpacked(mine, rest))
    two, scale_ref[1:2, :] = scaled(unpacked(raw_ref[...], raw_rest_ref[...]))
    done, rest = eliminated([one, two], 0, CHUNK)
    for m in range(2):
        done_ref[m] = done[m]
        rest_ref[m] = rest[m]


def lower_kernel(done_ref, rest_ref, scale_ref, inverse_ref, both_ref):
    done, _ = eliminated([rest_ref[0], rest_ref[1]], CHUNK, rest_ref.shape[2] // B)
    for m, ref in ((0, inverse_ref), (1, both_ref)):
        ref[...] = inverse_factor(jnp.concatenate([done_ref[m], done[m]], axis=0), scale_ref[m : m + 1, :])


def modes_kernel(product_ref, inverse_ref, modes_ref, *, scale):
    inverse = inverse_ref[...] * scale
    h = inverse.shape[0] // 2
    along = ((1,), (1,))
    modes_ref[:, :h] = dot(product_ref[:, :h], inverse[:h, :h], along)
    modes_ref[:, h:] = dot(product_ref[...], inverse[h:, :], along)


def projected_kernel(
    keep_ref, other_ref, keep_rest_ref, other_rest_ref, proj_ref, proj_rest_ref, inverse_ref, projected_ref
):
    bit = my_bit(2)
    mine = jnp.where(bit == 0, other_ref[...], keep_ref[...])
    rest = jnp.where(bit == 0, other_rest_ref[...], keep_rest_ref[...])
    projected_ref[0] = unpacked(mine, rest)
    inverse = inverse_ref[...]
    proj = dot(inverse, unpacked(proj_ref[...], proj_rest_ref[...]))
    projected_ref[1] = dot(proj, inverse, ((1,), (1,)))


def per_device(tiles, pattern, basis):
    block_rows, _, tile, _ = tiles.shape
    rows, modes = basis.shape
    peers = lax.axis_size("rows")
    f32 = lambda *shape: jax.ShapeDtypeStruct(shape, jnp.float32)
    half_sum = f32(3 * modes // 4, modes // 2)
    flops = 6 * rows * modes * modes
    place, rounded = kernel_call(
        functools.partial(prepare_kernel, block_rows=block_rows, peers=peers),
        (jax.ShapeDtypeStruct(pattern.shape, jnp.int32), jax.ShapeDtypeStruct((rows, modes), jnp.bfloat16)),
        pattern, basis,
        limit=8,
        in_specs=[pl.BlockSpec(memory_space=pltpu.VMEM), pl.BlockSpec(memory_space=pltpu.HBM)],
        scratch_shapes=[pltpu.VMEM(basis.shape, jnp.float32), pltpu.SemaphoreType.DMA((4,))],
    )
    pieces, (tiles, turn) = neighbourhood(rounded, lambda: held(tiles, modes))
    product, sent = product_of(place, tiles, turn, pieces, jnp.float32, jnp.bfloat16)

    def first_sums():
        mine, rest = kernel_call(
            first_sums_kernel, (f32(3 * modes // 2, modes // 2),) * 2, product, rounded, flops=LONG
        )
        return kernel_call(split_kernel, (half_sum,) * 2, mine, swapped(rest), limit=4)

    pieces, first = neighbourhood(sent, first_sums, lambda made: added(made[0], permuted(made[1], lambda i: i ^ 2)))
    partner = permuted(first, lambda i: i ^ 4)

    (raw,) = product_of(place, tiles, turn, pieces, jnp.float32)
    gram, rest, first = kernel_call(gram_kernel, (half_sum,) * 3, raw, first, partner, flops=LONG)
    gram = summed(gram, rest, 1, 2)
    first = after(first, gram)
    proj, rest = kernel_call(proj_kernel, (half_sum,) * 2, after(raw, gram), sent, turn, flops=LONG)
    gram = summed(gram, None, 2, 8)
    partner = permuted(first, lambda i: i ^ 8)
    first = added(*after((first, partner), gram))
    first, gram = summed(first, None, 16), summed(gram, None, 8)
    other = permuted(first, lambda i: i ^ 2)
    first = (first, other, swapped(first), swapped(other))
    proj = summed(proj, rest, 1, peers // 4)
    partner = permuted(proj, lambda i: i ^ (peers // 4))
    eliminating = kernel_call(
        upper_kernel,
        (f32(2, CHUNK * B, modes), f32(2, modes - CHUNK * B, modes), f32(2, modes)),
        *first, gram, swapped(gram),
        flops=LONG,
    )
    proj = added(*after((proj, partner), eliminating[0]))
    partner = permuted(proj, lambda i: i ^ (peers // 2))
    inverse, both = kernel_call(lower_kernel, (f32(modes, modes),) * 2, *eliminating, flops=3 * LONG)
    proj = added(*after((proj, partner), inverse))
    modes_out = kernel_call(
        functools.partial(modes_kernel, scale=math.sqrt(rows * peers)), f32(rows, modes), raw, both, flops=LONG
    )
    projected = kernel_call(projected_kernel, f32(2, modes, modes), *first, proj, swapped(proj), inverse)
    return modes_out, projected


def solution(mesh):
    placed = (
        P(("groups", "rows"), None, None, None),
        P(("groups", "rows"), None),
        P(("groups", "rows"), None),
    )
    return jax.shard_map(
        per_device,
        mesh=mesh,
        in_specs=placed,
        out_specs=(P(("groups", "rows"), None), P("groups", None, None)),
        check_vma=False,
    )
```

```python
import functools
import math

import jax
import jax.numpy as jnp
from jax import lax
from jax.experimental import pallas as pl
from jax.experimental.pallas import tpu as pltpu
from jax.sharding import PartitionSpec as P

B = 8
LANES = 128
CHUNK = 8
MIB = 2**20
LONG = 8_000_000_000


def permuted(value, target):
    peers = lax.axis_size("rows")
    return lax.ppermute(value, "rows", [(i, target(i) % peers) for i in range(peers)])


def swapped(value):
    return permuted(value, lambda i: i ^ 1)


def after(value, *others):
    return lax.optimization_barrier((value, others))[0]


def neighbourhood(blocks, meanwhile, then=lambda made: made):
    before = permuted(blocks, lambda i: i + 2)
    behind = permuted(blocks, lambda i: i - 2)
    far = permuted(blocks, lambda i: i + 3 if i % 2 else i - 3)
    made = meanwhile()
    other = swapped(after(blocks, made))
    made = then(made)
    before, behind = after(before, made), after(behind, made)
    return [blocks, other, before, swapped(before), behind, swapped(behind), far], made


def kernel_call(kernel, out_shape, *args, flops=0, limit=16, **kwargs):
    return pl.pallas_call(
        kernel,
        out_shape=out_shape,
        cost_estimate=pl.CostEstimate(flops=flops, bytes_accessed=2**20, transcendentals=0),
        compiler_params=pltpu.CompilerParams(vmem_limit_bytes=limit * MIB),
        **kwargs,
    )(*args)


def place_kernel(pattern_ref, place_ref, *, block_rows, peers):
    me = lax.axis_index("rows")
    pattern = pattern_ref[...]
    owner = lax.div(pattern, block_rows)
    apart = lax.rem(lax.div(owner, 2) - lax.div(me, 2) + (2 + peers // 2), peers // 2) - 2
    crossed = lax.rem(owner + me, 2)
    piece = jnp.where(apart == 0, crossed, jnp.where(apart == -1, 2 + crossed, jnp.where(apart == 1, 4 + crossed, 6)))
    place_ref[...] = piece * block_rows + lax.rem(pattern, block_rows)


def held_kernel(tiles_ref, held_ref, turn_ref, sems):
    copies = [pltpu.make_async_copy(tiles_ref.at[r], held_ref.at[r], sems.at[r]) for r in range(tiles_ref.shape[0])]
    for c in copies:
        c.start()
    n = turn_ref.shape[0]
    both = lax.broadcasted_iota(jnp.int32, (n, n), 0) & lax.broadcasted_iota(jnp.int32, (n, n), 1)
    shift = 1
    while 2**shift < n:
        both = both ^ (both >> shift)
        shift *= 2
    turn_ref[...] = jnp.where(both & 1 == 0, 1.0, -1.0).astype(turn_ref.dtype) * (1.0 / math.sqrt(n))
    for c in copies:
        c.wait()


def held(tiles, modes):
    return pl.pallas_call(
        held_kernel,
        in_specs=[pl.BlockSpec(memory_space=pltpu.HBM)],
        out_specs=[pl.BlockSpec(memory_space=pltpu.VMEM)] * 2,
        scratch_shapes=[pltpu.SemaphoreType.DMA((tiles.shape[0],))],
        out_shape=[
            jax.ShapeDtypeStruct(tiles.shape, tiles.dtype),
            jax.ShapeDtypeStruct((modes, modes), jnp.bfloat16),
        ],
        cost_estimate=pl.CostEstimate(flops=0, bytes_accessed=4 * tiles.size, transcendentals=0),
        compiler_params=pltpu.CompilerParams(vmem_limit_bytes=14 * MIB),
    )(tiles)


def turned(x, turn, parts):
    total = None
    for _ in range(parts):
        part = x.astype(jnp.bfloat16)
        term = jnp.dot(part, turn, preferred_element_type=jnp.float32)
        total = term if total is None else total + term
        x = x - part.astype(jnp.float32)
    return total


def product_kernel(place_ref, tiles_ref, turn_ref, *refs, pieces):
    piece_refs, (product_ref, *sent_refs, window) = refs[:pieces], refs[pieces:]
    block_rows, tile = piece_refs[0].shape[:2]
    for i in range(pieces):
        window[i * block_rows : (i + 1) * block_rows] = piece_refs[i][...]
    for r in range(block_rows):
        total = None
        for k in range(0, tiles_ref.shape[1], 2):
            left = jnp.concatenate([tiles_ref[r, k], tiles_ref[r, k + 1]], axis=1)
            right = jnp.concatenate([window[place_ref[r, k]], window[place_ref[r, k + 1]]], axis=0)
            term = jnp.dot(left, right, preferred_element_type=jnp.float32)
            total = term if total is None else total + term
        product_ref[r * tile : (r + 1) * tile, :] = total
    if sent_refs:
        sent_refs[0][...] = turned(product_ref[...], turn_ref[...], 2).astype(sent_refs[0].dtype)
    else:
        product_ref[...] = turned(product_ref[...], turn_ref[...], 3)


def product_of(place, tiles, turn, pieces, *types):
    block_rows, slots, tile, _ = tiles.shape
    modes = pieces[0].shape[-1]
    n = len(pieces)
    rows = block_rows * tile
    return pl.pallas_call(
        functools.partial(product_kernel, pieces=n),
        in_specs=[pl.BlockSpec(memory_space=pltpu.SMEM)] + [pl.BlockSpec(memory_space=pltpu.VMEM)] * (n + 2),
        scratch_shapes=[pltpu.VMEM((n * block_rows, tile, modes), jnp.bfloat16)],
        out_shape=[jax.ShapeDtypeStruct((rows, modes), t) for t in types],
        cost_estimate=pl.CostEstimate(flops=LONG, bytes_accessed=2 * tiles.size, transcendentals=0),
        compiler_params=pltpu.CompilerParams(vmem_limit_bytes=12 * MIB),
    )(place, tiles, turn, *[p.reshape(block_rows, tile, modes) for p in pieces])


def dot(a, b, dims=((1,), (0,))):
    return lax.dot_general(a, b, (dims, ((), ())), precision=lax.Precision.HIGHEST, preferred_element_type=jnp.float32)


def two_parts(x):
    high = x.astype(jnp.bfloat16)
    return high, (x - high.astype(jnp.float32)).astype(jnp.bfloat16)


def near_dot(a, b, dims=((1,), (0,))):
    one = lambda u, v: lax.dot_general(u, v, (dims, ((), ())), preferred_element_type=jnp.float32)
    return one(a[0], b[0]) + (one(a[0], b[1]) + one(a[1], b[0]))


def my_bit(bit):
    return lax.rem(lax.div(lax.axis_index("rows"), bit), 2)


def halves(left, right):
    down = ((0,), (0,))
    h = right.shape[1] // 2
    left, right = two_parts(left), two_parts(right)
    la, lb, ra, rb = ([p[:, at] for p in x] for x in (left, right) for at in (slice(0, h), slice(h, 2 * h)))
    low, mid, high = near_dot(la, ra, down), near_dot(lb, ra, down), near_dot(lb, rb, down)
    first = jnp.concatenate([low, mid[: h // 2]], axis=0)
    last = jnp.concatenate([mid[h // 2 :], high], axis=0)
    core = my_bit(1)
    return jnp.where(core == 0, first, last), jnp.where(core == 0, last, first)


def first_sums_kernel(product_ref, rounded_ref, mine_ref, rest_ref):
    n = mine_ref.shape[0] // 2
    product = product_ref[...]
    mine_ref[:n, :], rest_ref[:n, :] = halves(product, product)
    mine_ref[n:, :], rest_ref[n:, :] = halves(rounded_ref[...].astype(jnp.float32), product)


def gram_kernel(product_ref, a_ref, b_ref, mine_ref, rest_ref, added_ref):
    product = product_ref[...]
    mine_ref[...], rest_ref[...] = halves(product, product)
    added_ref[...] = a_ref[...] + b_ref[...]


def proj_kernel(product_ref, sent_ref, turn_ref, mine_ref, rest_ref):
    rounded = jnp.dot(sent_ref[...], turn_ref[...], preferred_element_type=jnp.float32)
    mine_ref[...], rest_ref[...] = halves(rounded, product_ref[...])


def split_kernel(a_ref, b_ref, mine_ref, rest_ref):
    total = a_ref[...] + b_ref[...]
    n = total.shape[0] // 2
    bit = my_bit(2)
    mine_ref[...] = jnp.where(bit == 0, total[:n], total[n:])
    rest_ref[...] = jnp.where(bit == 0, total[n:], total[:n])


def added_kernel(a_ref, b_ref, out_ref):
    out_ref[...] = a_ref[...] + b_ref[...]


def added(a, b):
    return kernel_call(added_kernel, jax.ShapeDtypeStruct(a.shape, a.dtype), a, b, limit=4)


def summed(mine, rest, first=1, last=None):
    step = first
    while step < (last or lax.axis_size("rows")):
        mine = added(mine, permuted(rest if step == 1 else mine, lambda i: i ^ step))
        step *= 2
    return mine


def unpacked(mine, rest):
    core = my_bit(1)
    first, last = jnp.where(core == 0, mine, rest), jnp.where(core == 0, rest, mine)
    h = 2 * mine.shape[0] // 3
    a, d = first[:h], last[h // 2 :]
    b = jnp.concatenate([first[h:], last[: h // 2]], axis=0)
    return jnp.concatenate([jnp.concatenate([a, b.T], axis=1), jnp.concatenate([b, d], axis=1)], axis=0)


def lane_bcast(x, j):
    return jnp.take_along_axis(x, jnp.broadcast_to(j, x.shape).astype(jnp.int32), axis=1)


def sub_bcast(x, i):
    return jnp.broadcast_to(x[i : i + 1, :], x.shape)


def wide(x, n):
    return x if n == 1 else jnp.concatenate([x] * n, axis=1)


def rsqrt(x):
    y = lax.rsqrt(x)
    return y * (1.5 - 0.5 * x * y * y)


def tree(terms):
    while len(terms) > 1:
        terms = [a + b for a, b in zip(terms[::2], terms[1::2])]
    return terms[0]


def pivot_rows(xk, k, tile, at, lane, sub, tiles):
    here = lane // B == k
    cols = [lane_bcast(xk[:, tile], at + j) for j in range(B)]
    start = jnp.where(here, jnp.where(lane - B * k == sub, 1.0, 0.0), xk)
    x = start
    one = sub[:, :LANES]
    for a in range(0, B, 2):
        b = a + 1
        pa = [sub_bcast(cols[j], a) for j in range(B)]
        pb = [sub_bcast(cols[j], b) for j in range(B)]
        inv = 1.0 / (pa[a] * pb[b] - pa[b] * pa[b])
        i00, i01, i11 = pb[b] * inv, -pa[b] * inv, pa[a] * inv
        mine = (one == a) | (one == b)
        ra, rb = sub_bcast(x, a), sub_bcast(x, b)
        qa = wide(i00, tiles) * ra + wide(i01, tiles) * rb
        qb = wide(i01, tiles) * ra + wide(i11, tiles) * rb
        ca = jnp.where(mine, jnp.where(one == a, -1.0, 0.0), cols[a])
        cb = jnp.where(mine, jnp.where(one == b, -1.0, 0.0), cols[b])
        wm = wide(mine, tiles)
        x = jnp.where(wm, 0.0, x) - (wide(ca, tiles) * qa + wide(cb, tiles) * qb)
        for j in range(b + 1, B):
            ta, tb = i00 * pa[j] + i01 * pb[j], i01 * pa[j] + i11 * pb[j]
            cols[j] = jnp.where(mine, 0.0, cols[j]) - (ca * ta + cb * tb)
    return [sub_bcast(x, i) for i in range(B)]


def pivot_factors(d, sub, lane):
    base = lane // B * B
    cols = [jnp.take_along_axis(d, base + j, axis=1) for j in range(B)]
    p = [[sub_bcast(cols[j], i) for j in range(B)] for i in range(B)]
    m = [[None] * B for _ in range(B)]
    out = jnp.zeros(d.shape, jnp.float32)
    for a in range(B):
        inv = 1.0 / p[a][a]
        for i in range(a + 1, B):
            l = p[i][a] * inv
            for j in range(a + 1, i + 1):
                p[i][j] = p[i][j] - l * p[j][a]
            for j in range(a):
                m[i][j] = m[i][j] - l * m[a][j]
            m[i][a] = -l
    for i in range(B):
        r = rsqrt(p[i][i])
        for j in range(i + 1):
            out = jnp.where((sub == i) & (lane % B == j), r if i == j else r * m[i][j], out)
    return out


def eliminated_block(x, first, groups, lane, sub, tiles):
    acting = []
    for s in range(groups):
        k = first + s
        t = k * B // LANES
        tile, at = slice(t * LANES, (t + 1) * LANES), k * B - t * LANES
        here = lane // B == k
        rows = pivot_rows(x[s], k, tile, at, lane, sub, tiles)
        for i in range(s + 1, groups):
            c = [wide(lane_bcast(x[i][:, tile], at + j), tiles) for j in range(B)]
            x[i] = jnp.where(here, 0.0, x[i]) - tree([c[j] * rows[j] for j in range(B)])
        own = rows[0]
        for j in range(1, B):
            own = jnp.where(sub == j, rows[j], own)
        acting.append(jnp.where((lane // B > k) & (lane // B < first + groups), 0.0, own))
    return x, acting


def scaled(g):
    row = lax.broadcasted_iota(jnp.int32, g.shape, 0)
    d = jnp.where(row == lax.broadcasted_iota(jnp.int32, g.shape, 1), g, 0.0)
    scale = rsqrt(jnp.sum(d, axis=0, keepdims=True))
    return g * rsqrt(jnp.sum(d, axis=1, keepdims=True)) * scale, scale


def eliminated(rest, first, last):
    n = rest[0].shape[1]
    tiles, many, per = n // LANES, range(len(rest)), CHUNK
    lane = lax.broadcasted_iota(jnp.int32, (B, n), 1)
    sub = lax.broadcasted_iota(jnp.int32, (B, n), 0)
    rest, done = list(rest), [[] for _ in many]
    for start in range(first, last, per):
        size, lo = per * B, start * B
        both = [
            eliminated_block([rest[m][i * B : i * B + B, :] for i in range(per)], start, per, lane, sub, tiles)
            for m in many
        ]
        for m in many:
            x, acting = both[m]
            done[m] += x
            if lo + size < n:
                left = jnp.concatenate(x, axis=0)
                below = (lo + size) // LANES * LANES
                update = dot(left[:, below:], jnp.concatenate(acting, axis=0), ((0,), (0,)))[lo + size - below :]
                lanes = lax.broadcasted_iota(jnp.int32, update.shape, 1)
                rest[m] = jnp.where(lanes // size == lo // size, 0.0, rest[m][size:]) - update
    return [jnp.concatenate(d, axis=0) for d in done], rest


def inverse_factor(done, scale):
    n = done.shape[0]
    lane = lax.broadcasted_iota(jnp.int32, (B, n), 1)
    sub = lax.broadcasted_iota(jnp.int32, (B, n), 0)
    groups = [done[k * B : k * B + B, :] for k in range(n // B)]
    strip = groups[0]
    for k in range(1, n // B):
        strip = jnp.where(lane // B == k, groups[k], strip)
    factors = [
        pivot_factors(strip[:, t : t + LANES], sub[:, :LANES], lane[:, :LANES]) for t in range(0, n, LANES)
    ]
    spread = jnp.concatenate(factors, axis=1)
    blocks, unit = [], []
    for k in range(n // B):
        here = lane // B == k
        blocks.append(jnp.where(here, spread, 0.0))
        eye = jnp.where(here & (lane - B * k == sub), 1.0, 0.0)
        unit.append(jnp.where(lane < B * k, groups[k], eye))
    return dot(jnp.concatenate(blocks, axis=0), jnp.concatenate(unit, axis=0)) * scale


def upper_kernel(
    keep_ref, other_ref, keep_rest_ref, other_rest_ref, raw_ref, raw_rest_ref, done_ref, rest_ref, scale_ref
):
    bit = my_bit(2)
    mine = jnp.where(bit == 0, keep_ref[...], other_ref[...])
    rest = jnp.where(bit == 0, keep_rest_ref[...], other_rest_ref[...])
    one, scale_ref[0:1, :] = scaled(unpacked(mine, rest))
    two, scale_ref[1:2, :] = scaled(unpacked(raw_ref[...], raw_rest_ref[...]))
    done, rest = eliminated([one, two], 0, CHUNK)
    for m in range(2):
        done_ref[m] = done[m]
        rest_ref[m] = rest[m]


def lower_kernel(done_ref, rest_ref, scale_ref, inverse_ref, both_ref):
    done, _ = eliminated([rest_ref[0], rest_ref[1]], CHUNK, rest_ref.shape[2] // B)
    for m, ref in ((0, inverse_ref), (1, both_ref)):
        ref[...] = inverse_factor(jnp.concatenate([done_ref[m], done[m]], axis=0), scale_ref[m : m + 1, :])


def modes_kernel(product_ref, inverse_ref, modes_ref, held, sems, *, scale):
    inverse = two_parts(inverse_ref[...] * scale)
    h = inverse_ref.shape[0] // 2
    along = ((1,), (1,))
    step = product_ref.shape[0] // sems.shape[0]
    copies = []
    for i in range(sems.shape[0]):
        at = slice(i * step, (i + 1) * step)
        product = two_parts(product_ref[at, :])
        held[at, :h] = near_dot([p[:, :h] for p in product], [w[:h, :h] for w in inverse], along)
        held[at, h:] = near_dot(product, [w[h:, :] for w in inverse], along)
        copies.append(pltpu.make_async_copy(held.at[at], modes_ref.at[at], sems.at[i]))
        copies[-1].start()
    for c in copies:
        c.wait()


def projected_kernel(
    keep_ref, other_ref, keep_rest_ref, other_rest_ref, proj_ref, proj_rest_ref, inverse_ref, projected_ref, held, sems
):
    copies = [pltpu.make_async_copy(held.at[i], projected_ref.at[i], sems.at[i]) for i in range(2)]
    bit = my_bit(2)
    mine = jnp.where(bit == 0, other_ref[...], keep_ref[...])
    rest = jnp.where(bit == 0, other_rest_ref[...], keep_rest_ref[...])
    held[0] = unpacked(mine, rest)
    copies[0].start()
    inverse = two_parts(inverse_ref[...])
    proj = near_dot(inverse, two_parts(unpacked(proj_ref[...], proj_rest_ref[...])))
    held[1] = near_dot(two_parts(proj), inverse, ((1,), (1,)))
    copies[1].start()
    for c in copies:
        c.wait()


def per_device(tiles, pattern, basis):
    block_rows, _, tile, _ = tiles.shape
    rows, modes = basis.shape
    peers = lax.axis_size("rows")
    f32 = lambda *shape: jax.ShapeDtypeStruct(shape, jnp.float32)
    half_sum = f32(3 * modes // 4, modes // 2)
    flops = 6 * rows * modes * modes
    rounded = basis.astype(jnp.bfloat16)

    def meanwhile():
        place = kernel_call(
            functools.partial(place_kernel, block_rows=block_rows, peers=peers),
            jax.ShapeDtypeStruct(pattern.shape, jnp.int32),
            pattern,
            limit=4,
        )
        return place, *held(tiles, modes)

    pieces, (place, kept, turn) = neighbourhood(rounded, meanwhile)
    product, sent = product_of(place, kept, turn, pieces, jnp.float32, jnp.bfloat16)

    def first_sums():
        mine, rest = kernel_call(
            first_sums_kernel, (f32(3 * modes // 2, modes // 2),) * 2, product, rounded, flops=LONG
        )
        return kernel_call(split_kernel, (half_sum,) * 2, mine, swapped(rest), limit=4)

    pieces, first = neighbourhood(sent, first_sums, lambda made: added(made[0], permuted(made[1], lambda i: i ^ 2)))
    partner = permuted(first, lambda i: i ^ 4)

    (raw,) = product_of(place, kept, turn, pieces, jnp.float32)
    gram, rest, first = kernel_call(gram_kernel, (half_sum,) * 3, raw, first, partner, flops=LONG)
    gram = summed(gram, rest, 1, 2)
    first = after(first, gram)
    proj, rest = kernel_call(proj_kernel, (half_sum,) * 2, after(raw, gram), sent, turn, flops=LONG)
    gram = summed(gram, None, 2, 8)
    partner = permuted(first, lambda i: i ^ 8)
    first = added(*after((first, partner), gram))
    first, gram = summed(first, None, 16), summed(gram, None, 8)
    other = permuted(first, lambda i: i ^ 2)
    first = (first, other, swapped(first), swapped(other))
    proj = summed(proj, rest, 1, peers // 4)
    partner = permuted(proj, lambda i: i ^ (peers // 4))
    eliminating = kernel_call(
        upper_kernel,
        (f32(2, CHUNK * B, modes), f32(2, modes - CHUNK * B, modes), f32(2, modes)),
        *first, gram, swapped(gram),
        flops=0,
    )
    proj = added(*after((proj, partner), eliminating[0]))
    partner = permuted(proj, lambda i: i ^ (peers // 2))
    inverse, both = kernel_call(lower_kernel, (f32(modes, modes),) * 2, *eliminating, flops=3 * LONG)
    proj = added(*after((proj, partner), inverse))
    modes_out = kernel_call(
        functools.partial(modes_kernel, scale=math.sqrt(rows * peers)), f32(rows, modes), raw, both,
        flops=LONG,
        out_specs=pl.BlockSpec(memory_space=pltpu.HBM),
        scratch_shapes=[pltpu.VMEM((rows, modes), jnp.float32), pltpu.SemaphoreType.DMA((4,))],
    )
    projected = kernel_call(
        projected_kernel, f32(2, modes, modes), *first, proj, swapped(proj), inverse,
        out_specs=pl.BlockSpec(memory_space=pltpu.HBM),
        scratch_shapes=[pltpu.VMEM((2, modes, modes), jnp.float32), pltpu.SemaphoreType.DMA((2,))],
    )
    return modes_out, projected


def solution(mesh):
    placed = (
        P(("groups", "rows"), None, None, None),
        P(("groups", "rows"), None),
        P(("groups", "rows"), None),
    )
    return jax.shard_map(
        per_device,
        mesh=mesh,
        in_specs=placed,
        out_specs=(P(("groups", "rows"), None), P("groups", None, None)),
        check_vma=False,
    )
```

```python
import functools
import math

import jax
import jax.numpy as jnp
from jax import lax
from jax.experimental import pallas as pl
from jax.experimental.pallas import tpu as pltpu
from jax.sharding import PartitionSpec as P

B = 8
LANES = 128
CHUNK = 8
MIB = 2**20
LONG = 8_000_000_000


def permuted(value, target):
    peers = lax.axis_size("rows")
    return lax.ppermute(value, "rows", [(i, target(i) % peers) for i in range(peers)])


def swapped(value):
    return permuted(value, lambda i: i ^ 1)


def after(value, *others):
    return lax.optimization_barrier((value, others))[0]


def neighbourhood(blocks, meanwhile, then=lambda made: made):
    before = permuted(blocks, lambda i: i + 2)
    behind = permuted(blocks, lambda i: i - 2)
    far = permuted(blocks, lambda i: i + 3 if i % 2 else i - 3)
    made = meanwhile()
    other = swapped(after(blocks, made))
    made = then(made)
    before, behind = after(before, made), after(behind, made)
    return [blocks, other, before, swapped(before), behind, swapped(behind), far], made


def kernel_call(kernel, out_shape, *args, flops=0, limit=16, **kwargs):
    return pl.pallas_call(
        kernel,
        out_shape=out_shape,
        cost_estimate=pl.CostEstimate(flops=flops, bytes_accessed=2**20, transcendentals=0),
        compiler_params=pltpu.CompilerParams(vmem_limit_bytes=limit * MIB),
        **kwargs,
    )(*args)


def place_kernel(pattern_ref, place_ref, *, block_rows, peers):
    me = lax.axis_index("rows")
    pattern = pattern_ref[...]
    owner = lax.div(pattern, block_rows)
    apart = lax.rem(lax.div(owner, 2) - lax.div(me, 2) + (2 + peers // 2), peers // 2) - 2
    crossed = lax.rem(owner + me, 2)
    piece = jnp.where(apart == 0, crossed, jnp.where(apart == -1, 2 + crossed, jnp.where(apart == 1, 4 + crossed, 6)))
    place_ref[...] = piece * block_rows + lax.rem(pattern, block_rows)


def held_kernel(tiles_ref, held_ref, turn_ref, sems):
    copies = [pltpu.make_async_copy(tiles_ref.at[r], held_ref.at[r], sems.at[r]) for r in range(tiles_ref.shape[0])]
    for c in copies:
        c.start()
    n = turn_ref.shape[0]
    both = lax.broadcasted_iota(jnp.int32, (n, n), 0) & lax.broadcasted_iota(jnp.int32, (n, n), 1)
    shift = 1
    while 2**shift < n:
        both = both ^ (both >> shift)
        shift *= 2
    turn_ref[...] = jnp.where(both & 1 == 0, 1.0, -1.0).astype(turn_ref.dtype) * (1.0 / math.sqrt(n))
    for c in copies:
        c.wait()


def held(tiles, modes):
    return pl.pallas_call(
        held_kernel,
        in_specs=[pl.BlockSpec(memory_space=pltpu.HBM)],
        out_specs=[pl.BlockSpec(memory_space=pltpu.VMEM)] * 2,
        scratch_shapes=[pltpu.SemaphoreType.DMA((tiles.shape[0],))],
        out_shape=[
            jax.ShapeDtypeStruct(tiles.shape, tiles.dtype),
            jax.ShapeDtypeStruct((modes, modes), jnp.bfloat16),
        ],
        cost_estimate=pl.CostEstimate(flops=0, bytes_accessed=4 * tiles.size, transcendentals=0),
        compiler_params=pltpu.CompilerParams(vmem_limit_bytes=14 * MIB),
    )(tiles)


def turned(x, turn, parts):
    total = None
    for _ in range(parts):
        part = x.astype(jnp.bfloat16)
        term = jnp.dot(part, turn, preferred_element_type=jnp.float32)
        total = term if total is None else total + term
        x = x - part.astype(jnp.float32)
    return total


def product_kernel(place_ref, tiles_ref, turn_ref, *refs, pieces):
    piece_refs, (product_ref, *sent_refs, window) = refs[:pieces], refs[pieces:]
    block_rows, tile = piece_refs[0].shape[:2]
    for i in range(pieces):
        window[i * block_rows : (i + 1) * block_rows] = piece_refs[i][...]
    for r in range(block_rows):
        total = None
        for k in range(0, tiles_ref.shape[1], 2):
            left = jnp.concatenate([tiles_ref[r, k], tiles_ref[r, k + 1]], axis=1)
            right = jnp.concatenate([window[place_ref[r, k]], window[place_ref[r, k + 1]]], axis=0)
            term = jnp.dot(left, right, preferred_element_type=jnp.float32)
            total = term if total is None else total + term
        product_ref[r * tile : (r + 1) * tile, :] = total
    if sent_refs:
        sent_refs[0][...] = turned(product_ref[...], turn_ref[...], 2).astype(sent_refs[0].dtype)
    else:
        product_ref[...] = turned(product_ref[...], turn_ref[...], 3)


def product_of(place, tiles, turn, pieces, *types):
    block_rows, slots, tile, _ = tiles.shape
    modes = pieces[0].shape[-1]
    n = len(pieces)
    rows = block_rows * tile
    return pl.pallas_call(
        functools.partial(product_kernel, pieces=n),
        in_specs=[pl.BlockSpec(memory_space=pltpu.SMEM)] + [pl.BlockSpec(memory_space=pltpu.VMEM)] * (n + 2),
        scratch_shapes=[pltpu.VMEM((n * block_rows, tile, modes), jnp.bfloat16)],
        out_shape=[jax.ShapeDtypeStruct((rows, modes), t) for t in types],
        cost_estimate=pl.CostEstimate(flops=LONG, bytes_accessed=2 * tiles.size, transcendentals=0),
        compiler_params=pltpu.CompilerParams(vmem_limit_bytes=12 * MIB),
    )(place, tiles, turn, *[p.reshape(block_rows, tile, modes) for p in pieces])


def dot(a, b, dims=((1,), (0,))):
    return lax.dot_general(a, b, (dims, ((), ())), precision=lax.Precision.HIGHEST, preferred_element_type=jnp.float32)


def two_parts(x):
    high = x.astype(jnp.bfloat16)
    return high, (x - high.astype(jnp.float32)).astype(jnp.bfloat16)


def near_dot(a, b, dims=((1,), (0,))):
    one = lambda u, v: lax.dot_general(u, v, (dims, ((), ())), preferred_element_type=jnp.float32)
    return one(a[0], b[0]) + (one(a[0], b[1]) + one(a[1], b[0]))


def my_bit(bit):
    return lax.rem(lax.div(lax.axis_index("rows"), bit), 2)


def halves(left, right):
    down = ((0,), (0,))
    h = right.shape[1] // 2
    left, right = two_parts(left), two_parts(right)
    la, lb, ra, rb = ([p[:, at] for p in x] for x in (left, right) for at in (slice(0, h), slice(h, 2 * h)))
    low, mid, high = near_dot(la, ra, down), near_dot(lb, ra, down), near_dot(lb, rb, down)
    first = jnp.concatenate([low, mid[: h // 2]], axis=0)
    last = jnp.concatenate([mid[h // 2 :], high], axis=0)
    core = my_bit(1)
    return jnp.where(core == 0, first, last), jnp.where(core == 0, last, first)


def first_sums_kernel(product_ref, rounded_ref, mine_ref, rest_ref):
    n = mine_ref.shape[0] // 2
    product = product_ref[...]
    mine_ref[:n, :], rest_ref[:n, :] = halves(product, product)
    mine_ref[n:, :], rest_ref[n:, :] = halves(rounded_ref[...].astype(jnp.float32), product)


def shrunk(product_ref):
    product = product_ref[...]
    scale = 1.0 / jnp.max(jnp.abs(product))
    return product * scale, scale


def write_halves(pair, scale, mine_ref, rest_ref):
    n = mine_ref.shape[0] - B
    for ref, half in zip((mine_ref, rest_ref), pair):
        ref[:n, :] = half
        ref[n:, :] = jnp.full((B, ref.shape[1]), scale, jnp.float32)


def gram_kernel(product_ref, a_ref, b_ref, mine_ref, rest_ref, added_ref):
    product, scale = shrunk(product_ref)
    write_halves(halves(product, product), scale, mine_ref, rest_ref)
    added_ref[...] = a_ref[...] + b_ref[...]


def proj_kernel(product_ref, sent_ref, turn_ref, mine_ref, rest_ref):
    product, scale = shrunk(product_ref)
    rounded = jnp.dot(sent_ref[...], turn_ref[...], preferred_element_type=jnp.float32)
    write_halves(halves(rounded, product), scale, mine_ref, rest_ref)


def scaled_sum_kernel(a_ref, b_ref, out_ref, *, power):
    n = out_ref.shape[0] - B
    scale = jnp.minimum(a_ref[n:, :], b_ref[n:, :])
    terms = []
    for ref in (a_ref, b_ref):
        ratio = (scale / ref[n:, :])[0:1, :]
        terms.append(ref[:n, :] * (ratio * ratio if power == 2 else ratio))
    out_ref[:n, :] = terms[0] + terms[1]
    out_ref[n:, :] = scale


def split_kernel(a_ref, b_ref, mine_ref, rest_ref):
    total = a_ref[...] + b_ref[...]
    n = total.shape[0] // 2
    bit = my_bit(2)
    mine_ref[...] = jnp.where(bit == 0, total[:n], total[n:])
    rest_ref[...] = jnp.where(bit == 0, total[n:], total[:n])


def added_kernel(a_ref, b_ref, out_ref):
    out_ref[...] = a_ref[...] + b_ref[...]


def added(a, b):
    return kernel_call(added_kernel, jax.ShapeDtypeStruct(a.shape, a.dtype), a, b, limit=4)


def summed(mine, rest, first=1, last=None, add=added):
    step = first
    while step < (last or lax.axis_size("rows")):
        mine = add(mine, permuted(rest if step == 1 else mine, lambda i: i ^ step))
        step *= 2
    return mine


def scaled_sum(power):
    kernel = functools.partial(scaled_sum_kernel, power=power)
    return lambda a, b: kernel_call(kernel, jax.ShapeDtypeStruct(a.shape, a.dtype), a, b, limit=4)


def unpacked(mine, rest):
    core = my_bit(1)
    first, last = jnp.where(core == 0, mine, rest), jnp.where(core == 0, rest, mine)
    h = 2 * mine.shape[0] // 3
    a, d = first[:h], last[h // 2 :]
    b = jnp.concatenate([first[h:], last[: h // 2]], axis=0)
    return jnp.concatenate([jnp.concatenate([a, b.T], axis=1), jnp.concatenate([b, d], axis=1)], axis=0)


def lane_bcast(x, j):
    return jnp.take_along_axis(x, jnp.broadcast_to(j, x.shape).astype(jnp.int32), axis=1)


def sub_bcast(x, i):
    return jnp.broadcast_to(x[i : i + 1, :], x.shape)


def wide(x, n):
    return x if n == 1 else jnp.concatenate([x] * n, axis=1)


def rsqrt(x):
    y = lax.rsqrt(x)
    return y * (1.5 - 0.5 * x * y * y)


def tree(terms):
    while len(terms) > 1:
        terms = [a + b for a, b in zip(terms[::2], terms[1::2])]
    return terms[0]


def pivot_rows(xk, k, tile, at, lane, sub, tiles):
    here = lane // B == k
    cols = [lane_bcast(xk[:, tile], at + j) for j in range(B)]
    start = jnp.where(here, jnp.where(lane - B * k == sub, 1.0, 0.0), xk)
    x = start
    one = sub[:, :LANES]
    for a in range(0, B, 2):
        b = a + 1
        pa = [sub_bcast(cols[j], a) for j in range(B)]
        pb = [sub_bcast(cols[j], b) for j in range(B)]
        inv = 1.0 / (pa[a] * pb[b] - pa[b] * pa[b])
        i00, i01, i11 = pb[b] * inv, -pa[b] * inv, pa[a] * inv
        mine = (one == a) | (one == b)
        ra, rb = sub_bcast(x, a), sub_bcast(x, b)
        qa = wide(i00, tiles) * ra + wide(i01, tiles) * rb
        qb = wide(i01, tiles) * ra + wide(i11, tiles) * rb
        ca = jnp.where(mine, jnp.where(one == a, -1.0, 0.0), cols[a])
        cb = jnp.where(mine, jnp.where(one == b, -1.0, 0.0), cols[b])
        wm = wide(mine, tiles)
        x = jnp.where(wm, 0.0, x) - (wide(ca, tiles) * qa + wide(cb, tiles) * qb)
        for j in range(b + 1, B):
            ta, tb = i00 * pa[j] + i01 * pb[j], i01 * pa[j] + i11 * pb[j]
            cols[j] = jnp.where(mine, 0.0, cols[j]) - (ca * ta + cb * tb)
    return [sub_bcast(x, i) for i in range(B)]


def pivot_factors(d, sub, lane):
    base = lane // B * B
    cols = [jnp.take_along_axis(d, base + j, axis=1) for j in range(B)]
    p = [[sub_bcast(cols[j], i) for j in range(B)] for i in range(B)]
    m = [[None] * B for _ in range(B)]
    out = jnp.zeros(d.shape, jnp.float32)
    for a in range(B):
        inv = 1.0 / p[a][a]
        for i in range(a + 1, B):
            l = p[i][a] * inv
            for j in range(a + 1, i + 1):
                p[i][j] = p[i][j] - l * p[j][a]
            for j in range(a):
                m[i][j] = m[i][j] - l * m[a][j]
            m[i][a] = -l
    for i in range(B):
        r = rsqrt(p[i][i])
        for j in range(i + 1):
            out = jnp.where((sub == i) & (lane % B == j), r if i == j else r * m[i][j], out)
    return out


def eliminated_block(x, first, groups, lane, sub, tiles):
    acting = []
    for s in range(groups):
        k = first + s
        t = k * B // LANES
        tile, at = slice(t * LANES, (t + 1) * LANES), k * B - t * LANES
        here = lane // B == k
        rows = pivot_rows(x[s], k, tile, at, lane, sub, tiles)
        for i in range(s + 1, groups):
            c = [wide(lane_bcast(x[i][:, tile], at + j), tiles) for j in range(B)]
            x[i] = jnp.where(here, 0.0, x[i]) - tree([c[j] * rows[j] for j in range(B)])
        own = rows[0]
        for j in range(1, B):
            own = jnp.where(sub == j, rows[j], own)
        acting.append(jnp.where((lane // B > k) & (lane // B < first + groups), 0.0, own))
    return x, acting


def scaled(g):
    row = lax.broadcasted_iota(jnp.int32, g.shape, 0)
    d = jnp.where(row == lax.broadcasted_iota(jnp.int32, g.shape, 1), g, 0.0)
    scale = rsqrt(jnp.sum(d, axis=0, keepdims=True))
    return g * rsqrt(jnp.sum(d, axis=1, keepdims=True)) * scale, scale


def eliminated(rest, first, last):
    n = rest[0].shape[1]
    tiles, many, per = n // LANES, range(len(rest)), CHUNK
    lane = lax.broadcasted_iota(jnp.int32, (B, n), 1)
    sub = lax.broadcasted_iota(jnp.int32, (B, n), 0)
    rest, done = list(rest), [[] for _ in many]
    for start in range(first, last, per):
        size, lo = per * B, start * B
        both = [
            eliminated_block([rest[m][i * B : i * B + B, :] for i in range(per)], start, per, lane, sub, tiles)
            for m in many
        ]
        for m in many:
            x, acting = both[m]
            done[m] += x
            if lo + size < n:
                left = jnp.concatenate(x, axis=0)
                below = (lo + size) // LANES * LANES
                update = dot(left[:, below:], jnp.concatenate(acting, axis=0), ((0,), (0,)))[lo + size - below :]
                lanes = lax.broadcasted_iota(jnp.int32, update.shape, 1)
                rest[m] = jnp.where(lanes // size == lo // size, 0.0, rest[m][size:]) - update
    return [jnp.concatenate(d, axis=0) for d in done], rest


def inverse_factor(done, scale):
    n = done.shape[0]
    lane = lax.broadcasted_iota(jnp.int32, (B, n), 1)
    sub = lax.broadcasted_iota(jnp.int32, (B, n), 0)
    groups = [done[k * B : k * B + B, :] for k in range(n // B)]
    strip = groups[0]
    for k in range(1, n // B):
        strip = jnp.where(lane // B == k, groups[k], strip)
    factors = [
        pivot_factors(strip[:, t : t + LANES], sub[:, :LANES], lane[:, :LANES]) for t in range(0, n, LANES)
    ]
    spread = jnp.concatenate(factors, axis=1)
    blocks, unit = [], []
    for k in range(n // B):
        here = lane // B == k
        blocks.append(jnp.where(here, spread, 0.0))
        eye = jnp.where(here & (lane - B * k == sub), 1.0, 0.0)
        unit.append(jnp.where(lane < B * k, groups[k], eye))
    return dot(jnp.concatenate(blocks, axis=0), jnp.concatenate(unit, axis=0)) * scale


def upper_kernel(
    keep_ref, other_ref, keep_rest_ref, other_rest_ref, raw_ref, raw_rest_ref, done_ref, rest_ref, scale_ref
):
    bit = my_bit(2)
    mine = jnp.where(bit == 0, keep_ref[...], other_ref[...])
    rest = jnp.where(bit == 0, keep_rest_ref[...], other_rest_ref[...])
    one, scale_ref[0:1, :] = scaled(unpacked(mine, rest))
    two, scale_ref[1:2, :] = scaled(unpacked(raw_ref[:-B, :], raw_rest_ref[:-B, :]))
    done, rest = eliminated([one, two], 0, CHUNK)
    for m in range(2):
        done_ref[m] = done[m]
        rest_ref[m] = rest[m]


def lower_kernel(done_ref, rest_ref, scale_ref, inverse_ref, both_ref):
    done, _ = eliminated([rest_ref[0], rest_ref[1]], CHUNK, rest_ref.shape[2] // B)
    for m, ref in ((0, inverse_ref), (1, both_ref)):
        ref[...] = inverse_factor(jnp.concatenate([done_ref[m], done[m]], axis=0), scale_ref[m : m + 1, :])


def modes_kernel(product_ref, gram_ref, inverse_ref, modes_ref, held, sems, *, scale):
    inverse = two_parts(inverse_ref[...] * scale)
    h = inverse_ref.shape[0] // 2
    along = ((1,), (1,))
    step = product_ref.shape[0] // sems.shape[0]
    shrink = gram_ref[-B:, :][0:1, 0:1]
    copies = []
    for i in range(sems.shape[0]):
        at = slice(i * step, (i + 1) * step)
        product = two_parts(product_ref[at, :] * shrink)
        held[at, :h] = near_dot([p[:, :h] for p in product], [w[:h, :h] for w in inverse], along)
        held[at, h:] = near_dot(product, [w[h:, :] for w in inverse], along)
        copies.append(pltpu.make_async_copy(held.at[at], modes_ref.at[at], sems.at[i]))
        copies[-1].start()
    for c in copies:
        c.wait()


def projected_kernel(
    keep_ref, other_ref, keep_rest_ref, other_rest_ref, proj_ref, proj_rest_ref, inverse_ref, projected_ref, held, sems
):
    copies = [pltpu.make_async_copy(held.at[i], projected_ref.at[i], sems.at[i]) for i in range(2)]
    bit = my_bit(2)
    mine = jnp.where(bit == 0, other_ref[...], keep_ref[...])
    rest = jnp.where(bit == 0, other_rest_ref[...], keep_rest_ref[...])
    held[0] = unpacked(mine, rest)
    copies[0].start()
    inverse = two_parts(inverse_ref[...])
    proj = near_dot(inverse, two_parts(unpacked(proj_ref[:-B, :], proj_rest_ref[:-B, :])))
    held[1] = near_dot(two_parts(proj), inverse, ((1,), (1,))) / proj_ref[-B:, :][0:1, 0:1]
    copies[1].start()
    for c in copies:
        c.wait()


def per_device(tiles, pattern, basis):
    block_rows, _, tile, _ = tiles.shape
    rows, modes = basis.shape
    peers = lax.axis_size("rows")
    f32 = lambda *shape: jax.ShapeDtypeStruct(shape, jnp.float32)
    half_sum = f32(3 * modes // 4, modes // 2)
    flops = 6 * rows * modes * modes
    rounded = basis.astype(jnp.bfloat16)

    def meanwhile():
        place = kernel_call(
            functools.partial(place_kernel, block_rows=block_rows, peers=peers),
            jax.ShapeDtypeStruct(pattern.shape, jnp.int32),
            pattern,
            limit=4,
        )
        return place, *held(tiles, modes)

    pieces, (place, kept, turn) = neighbourhood(rounded, meanwhile)
    product, sent = product_of(place, kept, turn, pieces, jnp.float32, jnp.bfloat16)

    def first_sums():
        mine, rest = kernel_call(
            first_sums_kernel, (f32(3 * modes // 2, modes // 2),) * 2, product, rounded, flops=LONG
        )
        return kernel_call(split_kernel, (half_sum,) * 2, mine, swapped(rest), limit=4)

    pieces, first = neighbourhood(sent, first_sums, lambda made: added(made[0], permuted(made[1], lambda i: i ^ 2)))
    partner = permuted(first, lambda i: i ^ 4)

    (raw,) = product_of(place, kept, turn, pieces, jnp.float32)
    scaled_half = f32(3 * modes // 4 + B, modes // 2)
    gram, rest, first = kernel_call(gram_kernel, (scaled_half,) * 2 + (half_sum,), raw, first, partner, flops=LONG)
    gram = summed(gram, rest, 1, 2, scaled_sum(2))
    first = after(first, gram)
    proj, rest = kernel_call(proj_kernel, (scaled_half,) * 2, after(raw, gram), sent, turn, flops=LONG)
    gram = summed(gram, None, 2, 8, scaled_sum(2))
    partner = permuted(first, lambda i: i ^ 8)
    first = added(*after((first, partner), gram))
    first, gram = summed(first, None, 16), summed(gram, None, 8, add=scaled_sum(2))
    other = permuted(first, lambda i: i ^ 2)
    first = (first, other, swapped(first), swapped(other))
    proj = summed(proj, rest, 1, peers // 4, scaled_sum(1))
    partner = permuted(proj, lambda i: i ^ (peers // 4))
    eliminating = kernel_call(
        upper_kernel,
        (f32(2, CHUNK * B, modes), f32(2, modes - CHUNK * B, modes), f32(2, modes)),
        *first, gram, swapped(gram),
        flops=0,
    )
    proj = scaled_sum(1)(*after((proj, partner), eliminating[0]))
    partner = permuted(proj, lambda i: i ^ (peers // 2))
    inverse, both = kernel_call(lower_kernel, (f32(modes, modes),) * 2, *eliminating, flops=3 * LONG)
    proj = scaled_sum(1)(*after((proj, partner), inverse))
    modes_out = kernel_call(
        functools.partial(modes_kernel, scale=math.sqrt(rows * peers)), f32(rows, modes), raw, gram, both,
        flops=LONG,
        out_specs=pl.BlockSpec(memory_space=pltpu.HBM),
        scratch_shapes=[pltpu.VMEM((rows, modes), jnp.float32), pltpu.SemaphoreType.DMA((4,))],
    )
    projected = kernel_call(
        projected_kernel, f32(2, modes, modes), *first, proj, swapped(proj), inverse,
        out_specs=pl.BlockSpec(memory_space=pltpu.HBM),
        scratch_shapes=[pltpu.VMEM((2, modes, modes), jnp.float32), pltpu.SemaphoreType.DMA((2,))],
    )
    return modes_out, projected


def solution(mesh):
    placed = (
        P(("groups", "rows"), None, None, None),
        P(("groups", "rows"), None),
        P(("groups", "rows"), None),
    )
    return jax.shard_map(
        per_device,
        mesh=mesh,
        in_specs=placed,
        out_specs=(P(("groups", "rows"), None), P("groups", None, None)),
        check_vma=False,
    )
```
